256 devices in a mesh: seq: 32 (over x, y, core), tensor: 8 (over z).
Axes of the slice: x: 4, y: 4, z: 8, core: 2. Of those that a mesh axis runs over, the one named last changes fastest.
Arguments:
- hidden_in: bfloat16 [2, 8192, 3584], P(None, 'seq', 'tensor'), may hold values from -6 to 6
- prompt_table: bfloat16 [16, 32, 3584], P(None, None, 'tensor'), may hold values from -6 to 6
- norm_gain: float32 [3584], replicated, may hold values from 0.1 to 1.9
- w_qkv: bfloat16 [3584, 9216], P(None, 'tensor'), may hold values from -4 to 4
- w_out: bfloat16 [7168, 3584], P(('tensor', 'seq')), may hold values from -0.5 to 0.5
- doc_lengths: int32 [2, 16], replicated, may hold values from 1 to 4352, 8192 in all within a row
- doc_tenant: int32 [2, 16], replicated, may hold values from 0 to 15
- prompt_lengths: int32 [2, 16], replicated, may hold values from 1 to 32
Outputs:
- block_out: bfloat16 [2, 8192, 3584], P(None, 'seq', 'tensor')
- tenant_loss: float32 [16], replicated
The draws below stay inside these ranges and needn't reach their ends.
Inputs may be any that keep to these rules, and one draw needn't show every extreme that they name: `doc_lengths`: each row's 16 lengths sum to 8192, and the longest is exactly 4352.
All inputs are finite; a program needn't handle non-finite values.
Results may differ from the reference program's by a relative error of at most 0.02.
Values may be sent and summed in bfloat16 or wider, within the bound.
A program may use at most 128 MiB of HBM per device.

```python
import math
import jax
import jax.numpy as jnp
import numpy as np
from jax import lax

D = 3584
HEADS = 56
KV_HEADS = 8
HEAD_DIM = 128
GROUP = 7
ROWS = 2
LEN = 8192
DOCS = 16
MOST_DOC = 4352
TENANTS = 16
PLEN = 32


def draw_hidden_in(key, part):
    key = jax.random.fold_in(key, 5)
    random_key = jax.random.fold_in(key, 0)
    random_part = jax.random.normal(random_key, (ROWS, LEN, D), jnp.float32)
    return jnp.clip(random_part, -6.0, 6.0).astype(jnp.bfloat16)


def draw_w_qkv(key, part):
    key = jax.random.fold_in(key, 9)
    base_key = jax.random.fold_in(key, 0)
    columns = KV_HEADS * (GROUP + 2) * HEAD_DIM
    weights_base = jnp.clip(jax.random.normal(base_key, (D, columns), jnp.float32), -6.0, 6.0) * D ** (-0.5)
    return weights_base.astype(jnp.bfloat16)


def plant(values, rng, smallest, high):
    index_at = [jax.random.randint(jax.random.fold_in(rng, axis), (), 0, length) for axis, length in enumerate(values.shape)]
    longest = values.shape.index(max(values.shape))
    neighbour = index_at[:longest] + [(index_at[longest] + 1) % values.shape[longest]] + index_at[longest + 1:]
    return values.at[tuple(index_at)].set(smallest).at[tuple(neighbour)].set(high)


def block_levels(key, dims, cuts, low, largest):
    def one(dim, blocks):
        heights = jax.random.uniform(jax.random.fold_in(jax.random.fold_in(key, 6), dim), (blocks,), jnp.float32, low / len(cuts), largest / len(cuts))
        return jnp.repeat(jnp.exp(heights), dims[dim] // blocks).reshape((-1,) + (1,) * (len(dims) - dim - 1))

    factor_of = one(*cuts[0])
    for cut in cuts[1:]:
        factor_of = factor_of * one(*cut)
    return factor_of


def length_profile(number_of, total, most, skew):
    loads = [(1 << 20) // math.isqrt(standing ** skew) + 1 for standing in range(2, number_of + 1)]
    rest, holding = total - most - (number_of - 1), [1] * (number_of - 1)
    while rest > 0:
        movable = [i for i in range(number_of - 1) if holding[i] < most]
        mass, left = sum([loads[i] for i in movable]), rest
        for i in movable:
            extra = min(most - holding[i], max(1, left * loads[i] // mass), rest)
            holding[i] = holding[i] + extra
            rest = rest - extra
    return np.array([most] + holding)


def ragged_sizes(rng, amount, total, reach, slope):
    if amount == 2:
        one = jax.random.randint(rng, (), max(1, total - reach), min(reach, total - 1) + 1)
        return jnp.stack([one, total - one])
    sizes = jnp.asarray(length_profile(amount, total, reach, slope), jnp.int32)
    couples = (amount - 1) // 2
    source_of, taker = sizes[1:1 + 2 * couples:2], sizes[2:2 + 2 * couples:2]
    margin = jnp.minimum(source_of - 1, reach - taker)
    moved = jax.random.randint(jax.random.fold_in(rng, 1), (couples,), 0, 1 << 20) % (margin + 1)
    sizes = sizes.at[1:1 + 2 * couples:2].set(source_of - moved).at[2:2 + 2 * couples:2].set(taker + moved)
    return sizes[jax.random.permutation(jax.random.fold_in(rng, 2), amount)]


def scatter_about(own_key, shape, scale, limit, pieces=(), kind=jnp.bfloat16):
    gain = block_levels(own_key, shape, pieces, -0.22, 0.18) if pieces else 1.0
    entries = jax.random.normal(own_key, shape, jnp.float32) * scale * gain
    return jnp.minimum(jnp.maximum(entries, -limit), limit).astype(kind)


def setup_inputs(seed: int = 0) -> dict:
    arg_keys = jax.random.split(jax.random.key(seed), 9)
    hidden_in = draw_hidden_in(jax.random.fold_in(arg_keys[8], 71), 0)
    prompt_table = scatter_about(arg_keys[1], (TENANTS, PLEN, D), 1.0, 6.0, ((2, 8),))
    norm_gain = jnp.clip(1.0 + 0.18 * jax.random.normal(arg_keys[2], (D,), jnp.float32), 0.1, 1.9)
    w_qkv = draw_w_qkv(jax.random.fold_in(arg_keys[8], 71), 0)
    w_out = scatter_about(arg_keys[4], (HEADS * HEAD_DIM, D), HEAD_DIM ** -0.5, 0.5, ((0, 256),))
    doc_lengths = jax.vmap(lambda own: ragged_sizes(own, DOCS, LEN, MOST_DOC, 2))(jax.random.split(arg_keys[5], ROWS)).reshape((ROWS, DOCS)).astype(jnp.int32)
    doc_tenant = plant(jax.random.randint(arg_keys[6], (ROWS, DOCS), 0, TENANTS), jax.random.fold_in(arg_keys[6], 1), 0, TENANTS - 1).astype(jnp.int32)
    prompt_lengths = plant(jax.random.randint(arg_keys[7], (ROWS, DOCS), 1, PLEN + 1), jax.random.fold_in(arg_keys[7], 1), 1, PLEN).astype(jnp.int32)
    return dict(hidden_in=hidden_in, prompt_table=prompt_table, norm_gain=norm_gain, w_qkv=w_qkv, w_out=w_out, doc_lengths=doc_lengths, doc_tenant=doc_tenant, prompt_lengths=prompt_lengths)


THETA = 5000000.0
EPS = 1e-05

def doc_table(lengths, tenants, prompt_len, token_pos):
    starts = jnp.cumsum(lengths) - lengths
    covered = (starts[None, :] <= token_pos[:, None]).astype(jnp.int32)
    doc_ids = lax.optimization_barrier(jnp.sum(covered, axis=1)) - 1
    onehot = (doc_ids[:, None] == jnp.arange(lengths.shape[0], dtype=jnp.int32)[None, :]).astype(jnp.int32)
    doc_begin = lax.optimization_barrier(jnp.sum(onehot * starts[None, :], axis=1))
    tenant = lax.optimization_barrier(jnp.sum(onehot * tenants[None, :], axis=1))
    head_len = lax.optimization_barrier(jnp.sum(onehot * prompt_len[None, :], axis=1))
    within = token_pos - doc_begin
    return (doc_ids, within, tenant, within < head_len)

def rotate(values_in, within):
    half_dim = values_in.shape[-1] // 2
    inverse_freq = THETA ** (-jnp.arange(half_dim, dtype=jnp.float32) / half_dim)
    angles = within.astype(jnp.float32)[..., None] * inverse_freq
    angles = angles.reshape(within.shape + (1,) * (values_in.ndim - within.ndim - 1) + (half_dim,))
    cosine = jnp.cos(angles)
    sine_part = jnp.sin(angles)
    first_part = values_in[..., :half_dim]
    second = values_in[..., half_dim:]
    return jnp.concatenate([first_part * cosine - second * sine_part, second * cosine + first_part * sine_part], axis=-1)

def reference(hidden_in, prompt_table, norm_gain, w_qkv, w_out, doc_lengths, doc_tenant, prompt_lengths):
    query_block = math.gcd(LEN, 256)

    def one_row(row_args):
        hidden_row, lengths, tenants, prompt_len = row_args
        token_pos = jnp.arange(LEN, dtype=jnp.int32)
        doc_ids, within, tenant, prompt = doc_table(lengths, tenants, prompt_len, token_pos)
        lookup = prompt_table[tenant, jnp.minimum(within, PLEN - 1)]
        embedded = jnp.where(prompt[:, None], lookup, hidden_row)
        wide = embedded.astype(jnp.float32)
        scale = lax.rsqrt(lax.optimization_barrier(jnp.mean(wide * wide, axis=1, keepdims=True)) + EPS)
        normed = (wide * scale * norm_gain[None, :]).astype(jnp.bfloat16)
        projected = jnp.dot(normed, w_qkv, preferred_element_type=jnp.float32)
        projected = projected.reshape(LEN, KV_HEADS, GROUP + 2, HEAD_DIM)
        query = rotate(projected[:, :, :GROUP], within).astype(jnp.bfloat16)
        keys_all = rotate(projected[:, :, GROUP], within).astype(jnp.bfloat16)
        values_all = projected[:, :, GROUP + 1].astype(jnp.bfloat16)

        def attend_block(block_start):
            query_part = lax.dynamic_slice_in_dim(query, block_start, query_block, 0)
            query_docs = lax.dynamic_slice_in_dim(doc_ids, block_start, query_block, 0)
            query_pos = block_start + jnp.arange(query_block, dtype=jnp.int32)
            scores = jnp.einsum('qgjh,kgh->gjqk', query_part.astype(jnp.float32), keys_all.astype(jnp.float32)) * HEAD_DIM ** (-0.5)
            allowed = (query_docs[:, None] == doc_ids[None, :]) & (token_pos[None, :] <= query_pos[:, None])
            scores = jnp.where(allowed, scores, -1e+30)
            row_max = lax.optimization_barrier(jnp.max(scores, axis=3, keepdims=True))
            weights = jnp.where(allowed, jnp.exp(scores - row_max), 0.0)
            totals = lax.optimization_barrier(jnp.sum(weights, axis=3))
            weights_bf = lax.optimization_barrier(weights.astype(jnp.bfloat16))
            summed = jnp.einsum('gjqk,kgh->qgjh', weights_bf.astype(jnp.float32), values_all.astype(jnp.float32))
            return (summed / jnp.transpose(totals, (2, 0, 1))[..., None]).astype(jnp.bfloat16)
        block_starts = jnp.arange(LEN // query_block, dtype=jnp.int32) * query_block
        context = lax.map(attend_block, block_starts).reshape(LEN, HEADS * HEAD_DIM)
        delta = jnp.dot(context, w_out, preferred_element_type=jnp.float32)
        row_out = (wide + delta).astype(jnp.bfloat16)
        proxy = jnp.where(prompt, 0.0, lax.optimization_barrier(jnp.sum(delta * delta, axis=1)) / D)
        owner = (tenant[:, None] == jnp.arange(TENANTS, dtype=jnp.int32)[None, :]).astype(jnp.float32)
        return (row_out, lax.optimization_barrier(jnp.sum(owner * proxy[:, None], axis=0)))
    block_out, row_sums = lax.map(one_row, (hidden_in, doc_lengths, doc_tenant, prompt_lengths))
    return (block_out, lax.optimization_barrier(jnp.sum(row_sums, axis=0)))
```

```python
import functools

import jax
import jax.numpy as jnp
import numpy as np
from jax import lax
from jax.experimental import pallas as pl
from jax.experimental.pallas import tpu as pltpu
from jax.sharding import PartitionSpec as P

D = 3584
HEAD_DIM = 128
GROUP = 7
TENANTS = 16
PLEN = 32
THETA = 5000000.0
EPS = 1e-05

SEQ = 32
RING = 8
POS = 256
FEAT = 448
HALF = POS // 2
WIDE = 2 * FEAT
SUB = HALF // 2
COLS = (GROUP + 2) * HEAD_DIM
SHARD = 28
SLOT = 32
DEPTH = SEQ * SLOT
WINDOW = 9
QSCALE = HEAD_DIM**-0.5 * 1.4426950408889634
LOW = -1e30
MESH = pl.DeviceIdType.MESH
F32 = jnp.float32
BF16 = jnp.bfloat16


def dot(a, b):
    return jnp.dot(a, b, preferred_element_type=F32)


def place():
    return lax.axis_index("seq"), lax.axis_index("tensor")


def greet(peers):
    barrier = pltpu.get_barrier_semaphore()
    for peer in peers:
        pl.semaphore_signal(barrier, inc=1, device_id=peer, device_id_type=MESH)
    pl.semaphore_wait(barrier, len(peers))


def ring_peers():
    s, z = place()
    return [(s, lax.rem(z + 1, RING)), (s, lax.rem(z + RING - 1, RING))]


def push(src, dst, send, recv, peer):
    return pltpu.make_async_remote_copy(
        src_ref=src, dst_ref=dst, send_sem=send, recv_sem=recv, device_id=peer, device_id_type=MESH
    )


def unpack(x):
    return jnp.concatenate([x[:, :FEAT], x[:, FEAT:]], axis=0)


def pack(x):
    return jnp.concatenate([x[:HALF], x[HALF:]], axis=1)


def feature_steps(x, buf, send, recv, absorb):
    s, z = place()
    peers = ring_peers()

    def moved(way, hop, sub, mine):
        step = 1 if way == 0 else RING - 1
        origin = lax.rem(z + (RING - step) * (hop - 1 if mine else hop), RING)
        rows = pl.ds(sub * SUB, SUB)
        src = x.at[rows] if mine and hop == 1 else buf.at[origin, rows]
        index = (way, hop - 1, sub)
        return push(src, buf.at[origin, rows], send.at[index], recv.at[index], peers[way])

    sent = []

    def go(way, hop, sub):
        if hop == 4 and sub != way:
            return
        copy = moved(way, hop, sub, True)
        copy.start()
        sent.append(copy)

    for sub in range(2):
        for way in range(2):
            go(way, 1, sub)
    yield
    absorb(x[...], z)
    yield
    for hop in range(1, 4):
        for sub in range(2):
            for way in range(2):
                moved(way, hop, sub, False).wait_recv()
                go(way, hop + 1, sub)
            yield
        absorb(buf[lax.rem(z + RING - hop, RING)], lax.rem(z + RING - hop, RING))
        yield
        absorb(buf[lax.rem(z + hop, RING)], lax.rem(z + hop, RING))
        yield
    for way in range(2):
        moved(way, 4, way, False).wait_recv()
    yield
    absorb(buf[lax.rem(z + 4, RING)], lax.rem(z + 4, RING))
    yield
    for copy in sent:
        copy.wait_send()


class Projection:
    def __init__(self, gain, w, cos, sin, wbuf, wsem, acc, ssq):
        self.gain, self.w, self.cos, self.sin = gain, w, cos, sin
        self.wbuf, self.wsem, self.acc, self.ssq = wbuf, wsem, acc, ssq

    def fetch(self):
        z = place()[1]
        for away in (0, 7, 1, 6, 2, 5, 3, 4):
            self.copy(lax.rem(z + away, RING)).start()

    def copy(self, origin):
        return pltpu.make_async_copy(
            self.w.at[pl.ds(origin * FEAT, FEAT)], self.wbuf.at[origin], self.wsem.at[origin]
        )

    def clear(self):
        self.acc[...] = jnp.zeros_like(self.acc)
        self.ssq[...] = jnp.zeros_like(self.ssq)

    def absorb(self, x, origin):
        self.copy(origin).wait()
        wide = unpack(x).astype(F32)
        self.ssq[...] += jnp.sum(wide * wide, axis=1, keepdims=True)
        scaled = (wide * self.gain[origin]).astype(BF16)
        self.acc[...] += dot(scaled, self.wbuf[origin])

    def finish(self, q, kv):
        scale = lax.rsqrt(self.ssq[:, :1] / D + EPS)
        cos, sin = self.cos[...], self.sin[...]

        def rotated(n):
            part = self.acc[:, n * HEAD_DIM : (n + 1) * HEAD_DIM] * scale
            return part * cos + pltpu.roll(part, HEAD_DIM // 2, 1) * sin

        for n in range(GROUP):
            q[n] = (rotated(n) * QSCALE).astype(BF16)
        kv[:HEAD_DIM] = rotated(GROUP).T.astype(BF16)
        value = (self.acc[:, (GROUP + 1) * HEAD_DIM :] * scale).astype(BF16)
        kv[HEAD_DIM:] = pack(value)


def plane_peers():
    s, z = place()
    x, y, c = s // 8, lax.rem(s // 2, 4), lax.rem(s, 2)

    def at(a, b):
        dx, dy = a * (1 - c) + b * c, a * c + b * (1 - c)
        return lax.rem(x + dx, 4) * 8 + lax.rem(y + dy, 4) * 2 + c

    return at, [(at(1, 0), z), (at(3, 0), z)], [(at(0, 1), z), (at(0, 3), z)], (s + 1 - 2 * c, z)


def key_steps(own, everyone, send, recv, local):
    at, first, second, sibling = plane_peers()
    s, _ = place()
    sent = []
    halves = (pl.ds(0, HALF), pl.ds(HALF, HALF))
    back = (3, 1)

    def give(slot, rows, index, peer, src=None):
        ref = everyone.at[slot, rows] if rows is not None else everyone.at[slot]
        return push(ref if src is None else src, ref, send.at[index], recv.at[index], peer)

    def go(*args, **kwargs):
        copy = give(*args, **kwargs)
        copy.start()
        sent.append(copy)

    keep = pltpu.make_async_copy(own, everyone.at[s], local)
    keep.start()
    for way in range(2):
        go(s, None, way, first[way], src=own)
    for way in range(2):
        go(s, None, 4 + way, second[way], src=own)
    go(s, None, 20, sibling, src=own)
    yield

    def spread(a, slot):
        for way in range(2):
            go(slot, None, 4 + 4 * a + way, second[way])
        go(slot, None, 20 + 4 * a, sibling)

    for way in range(2):
        slot = at(back[way], 0)
        give(slot, None, way, first[way]).wait_recv()
        go(slot, halves[way], 2 + way, first[way])
        spread(back[way], slot)
    yield
    slot = at(2, 0)
    for way in range(2):
        give(slot, halves[way], 2 + way, first[way]).wait_recv()
    spread(2, slot)
    yield
    for a in (0, 3, 1, 2):
        for way in range(2):
            slot = at(a, back[way])
            give(slot, None, 4 + 4 * a + way, second[way]).wait_recv()
            go(slot, halves[way], 6 + 4 * a + way, second[way])
            go(slot, None, 20 + 4 * a + back[way], sibling)
        yield
    for a in (0, 3, 1, 2):
        slot = at(a, 2)
        for way in range(2):
            give(slot, halves[way], 6 + 4 * a + way, second[way]).wait_recv()
        go(slot, None, 20 + 4 * a + 2, sibling)
        yield
    c = lax.rem(s, 2)
    x, y = s // 8, lax.rem(s // 2, 4)
    for a in range(4):
        for b in range(4):
            dx, dy = a * c + b * (1 - c), a * (1 - c) + b * c
            slot = lax.rem(x + dx, 4) * 8 + lax.rem(y + dy, 4) * 2 + 1 - c
            give(slot, None, 20 + 4 * a + b, sibling).wait_recv()
    keep.wait()
    for copy in sent:
        copy.wait_send()
    yield


KEY_SEMS = 36


def attend(step, q, kv, begin, acc, top):
    s, _ = place()
    last = s - 2 * step
    low = jnp.maximum(last - 1, 0)
    key_pos = low * POS + lax.broadcasted_iota(jnp.int32, (POS, 2 * POS), 1)
    query_pos = s * POS + lax.broadcasted_iota(jnp.int32, (POS, 2 * POS), 0)
    allowed = (key_pos >= begin) & (key_pos <= jnp.minimum(query_pos, last * POS + POS - 1))
    bias = jnp.where(allowed, 0.0, LOW)
    blocks = kv[pl.ds(low, 2)]
    keys = jnp.concatenate([blocks[0, :HEAD_DIM], blocks[1, :HEAD_DIM]], axis=1)
    values = [blocks[n, HEAD_DIM:, m * HEAD_DIM : (m + 1) * HEAD_DIM] for n in (0, 1) for m in (0, 1)]
    values = jnp.concatenate(values, axis=0)
    values = jnp.concatenate([values, jnp.ones_like(values)], axis=1)
    for n in range(GROUP):
        scores = dot(q[n], keys) + bias
        old = top[n]
        new = jnp.maximum(old, jnp.max(scores, axis=1, keepdims=True))
        weights = jnp.exp2(scores - jnp.concatenate([new] * 4, axis=1)).astype(BF16)
        rescale = jnp.exp2(old - new)
        acc[n] = acc[n] * jnp.concatenate([rescale] * 2, axis=1) + dot(weights, values)
        top[n] = new


def start_attend(acc, top):
    acc[...] = jnp.zeros_like(acc)
    top[...] = jnp.full_like(top, LOW)


def finish_attend(acc, ctx):
    for n in range(GROUP):
        both = acc[n]
        ctx[:, n * HEAD_DIM : (n + 1) * HEAD_DIM] = (both[:, :HEAD_DIM] / both[:, HEAD_DIM:]).astype(BF16)


class Sums:
    def __init__(self, w, wbuf, wsem, out, came, send, recv):
        self.w, self.wbuf, self.wsem = w, wbuf, wsem
        self.out, self.came, self.send, self.recv = out, came, send, recv
        self.peers = ring_peers()
        self.sent = []

    def copy(self, owner):
        return pltpu.make_async_copy(self.w.at[:, owner], self.wbuf.at[owner], self.wsem.at[owner])

    def fetch(self):
        z = place()[1]
        for away in (4, 3, 5, 2, 6, 1, 7, 0):
            self.copy(lax.rem(z + away, RING)).start()

    def part(self, owner):
        self.copy(owner).wait()
        return pack(dot(self.ctx, self.wbuf[owner].reshape(DEPTH, FEAT)))

    def move(self, way, k, sub):
        rows = pl.ds(sub * SUB, SUB)
        index = (way, k, sub)
        return push(
            self.out.at[way, k, rows], self.came.at[way, k, rows],
            self.send.at[index], self.recv.at[index], self.peers[way],
        )

    def ship(self, way, k, sub, value):
        self.out[way, k, pl.ds(sub * SUB, SUB)] = value.astype(BF16)
        copy = self.move(way, k, sub)
        copy.start()
        self.sent.append(copy)

    def arrived(self, way, k, sub):
        self.move(way, k, sub).wait_recv()
        return self.came[way, k, pl.ds(sub * SUB, SUB)].astype(F32)

    def steps(self, ctx, perm):
        z = place()[1]
        self.ctx = dot(ctx[...], perm[...]).astype(BF16)
        value = self.part(lax.rem(z + 4, RING))
        for way in range(2):
            self.ship(way, 0, way, value[way * SUB : (way + 1) * SUB])
        yield
        for k in range(1, 4):
            value = [self.part(lax.rem(z + 4 - k, RING)), self.part(lax.rem(z + 4 + k, RING))]
            for turn in range(2):
                for way in range(2):
                    sub = turn ^ way if k == 1 else turn
                    piece = value[way][sub * SUB : (sub + 1) * SUB]
                    if k > 1 or sub == way:
                        piece = piece + self.arrived(way, k - 1, sub)
                    self.ship(way, k, sub, piece)
                yield
        value = self.part(z)
        got = []
        for sub in range(2):
            piece = value[sub * SUB : (sub + 1) * SUB]
            for way in range(2):
                piece = piece + self.arrived(way, 3, sub)
            got.append(piece)
        self.delta = jnp.concatenate(got, axis=0)
        for copy in self.sent:
            copy.wait_send()
        yield


def emit(sums, emb, owner, out, loss):
    delta = unpack(sums.delta)
    out[...] = (unpack(emb[...]).astype(F32) + delta).astype(BF16)
    proxy = jnp.sum(delta * delta, axis=1, keepdims=True) / D
    lanes = lax.broadcasted_iota(jnp.int32, (POS, HEAD_DIM), 1)
    total = jnp.sum(jnp.where(owner[...] == lanes, proxy, 0.0), axis=0, keepdims=True)
    loss[...] = jnp.broadcast_to(total, loss.shape)


def loss_groups():
    s, z = place()
    x, y, c = s // 8, lax.rem(s // 2, 4), lax.rem(s, 2)
    xc = x * 2 + c
    return [
        (z, 8, lambda n: (s, n)),
        (xc, 8, lambda n: ((n // 2) * 8 + y * 2 + lax.rem(n, 2), z)),
        (y, 4, lambda n: (x * 8 + n * 2 + c, z)),
    ]


def loss_peers():
    return [who(lax.rem(me + j, n)) for me, n, who in loss_groups() for j in range(1, n)]


def loss_total(value, slots, send, recv):
    for stage, (me, n, who) in enumerate(loss_groups()):
        slots[stage, me] = value
        sent = []
        for j in range(1, n):
            ref = slots.at[stage, me]
            copy = push(ref, ref, send.at[stage, j], recv.at[stage, j], who(lax.rem(me + j, n)))
            copy.start()
            sent.append(copy)
        for j in range(1, n):
            ref = slots.at[stage, lax.rem(me + n - j, n)]
            push(ref, ref, send.at[stage, j], recv.at[stage, j], who(lax.rem(me + j, n))).wait_recv()
        value = slots[stage, 0]
        for j in range(1, n):
            value = value + slots[stage, j]
        for copy in sent:
            copy.wait_send()
    return value


def alternate(*many):
    many = list(many)
    while many:
        for one in list(many):
            try:
                next(one)
            except StopIteration:
                many.remove(one)


RING_SEMS = pltpu.SemaphoreType.DMA((2, 4, 2))
FEATURE_SCRATCH = [
    pltpu.VMEM((RING, HALF, WIDE), BF16),
    pltpu.VMEM((RING, FEAT, COLS), BF16),
    pltpu.SemaphoreType.DMA((RING,)),
    pltpu.VMEM((POS, COLS), F32),
    pltpu.VMEM((POS, HEAD_DIM), F32),
    RING_SEMS,
    RING_SEMS,
]
KEY_SCRATCH = [
    pltpu.SemaphoreType.DMA((KEY_SEMS,)),
    pltpu.SemaphoreType.DMA((KEY_SEMS,)),
    pltpu.SemaphoreType.DMA,
]
SUM_SCRATCH = [
    pltpu.VMEM((RING, SEQ, SLOT, FEAT), BF16),
    pltpu.SemaphoreType.DMA((RING,)),
    pltpu.VMEM((2, 4, HALF, WIDE), BF16),
    pltpu.VMEM((2, 4, HALF, WIDE), BF16),
    RING_SEMS,
    RING_SEMS,
]
ATTEND_SCRATCH = [
    pltpu.VMEM((GROUP, POS, 2 * HEAD_DIM), F32),
    pltpu.VMEM((GROUP, POS, HEAD_DIM), F32),
]
VM = pl.BlockSpec(memory_space=pltpu.VMEM)
ANY = pl.BlockSpec(memory_space=pl.ANY)
Q_SHAPE = jax.ShapeDtypeStruct((GROUP, POS, HEAD_DIM), BF16)
KV_SHAPE = jax.ShapeDtypeStruct((POS, 2 * HEAD_DIM), BF16)
KEYS_SHAPE = jax.ShapeDtypeStruct((SEQ, POS, 2 * HEAD_DIM), BF16)
CTX_SHAPE = jax.ShapeDtypeStruct((POS, GROUP * HEAD_DIM), BF16)
OUT_SHAPE = jax.ShapeDtypeStruct((POS, FEAT), BF16)
LOSS_SHAPE = jax.ShapeDtypeStruct((8, HEAD_DIM), F32)


def project_kernel(x, gain, w, cos, sin, q, kv, buf, wbuf, wsem, acc, ssq, send, recv):
    proj = Projection(gain, w, cos, sin, wbuf, wsem, acc, ssq)
    proj.fetch()
    greet(ring_peers())
    proj.clear()
    alternate(feature_steps(x, buf, send, recv, proj.absorb))
    proj.finish(q, kv)


def project_keys_kernel(
    x, gain, w, cos, sin, own, q, kv, everyone,
    buf, wbuf, wsem, acc, ssq, send, recv, ksend, krecv, klocal,
):
    proj = Projection(gain, w, cos, sin, wbuf, wsem, acc, ssq)
    proj.fetch()
    _, first, second, sibling = plane_peers()
    greet(ring_peers() + first + second + [sibling])
    proj.clear()
    alternate(
        feature_steps(x, buf, send, recv, proj.absorb),
        key_steps(own, everyone, ksend, krecv, klocal),
    )
    proj.finish(q, kv)


def keys_kernel(own, everyone, ksend, krecv, klocal):
    _, first, second, sibling = plane_peers()
    greet(first + second + [sibling])
    alternate(key_steps(own, everyone, ksend, krecv, klocal))


def attend_kernel(count, q0, q1, kv0, kv1, begin0, begin1, ctx0, ctx1, acc, top):
    for row, (q, kv, begin, ctx) in enumerate(((q0, kv0, begin0, ctx0), (q1, kv1, begin1, ctx1))):
        start_attend(acc, top)

        def step(n, carry, q=q, kv=kv, begin=begin):
            attend(n, q, kv, begin[...], acc, top)
            return carry

        lax.fori_loop(0, count[row], step, 0)
        finish_attend(acc, ctx)


def sums_kernel(ctx, perm, w, emb, owner, out, loss, *scratch):
    sums = Sums(w, *scratch)
    sums.fetch()
    greet(sums.peers)
    alternate(sums.steps(ctx, perm))
    emit(sums, emb, owner, out, loss)


def last_kernel(ctx, perm, w, emb, owner, other, out, loss, *scratch):
    *scratch, slots, lsend, lrecv = scratch
    sums = Sums(w, *scratch)
    sums.fetch()
    greet(loss_peers())
    alternate(sums.steps(ctx, perm))
    emit(sums, emb, owner, out, loss)
    loss[...] = loss_total(loss[...] + other[...], slots, lsend, lrecv)


def call(kernel, ident, out_shape, in_specs, out_specs, scratch, mib, flops):
    return pl.pallas_call(
        kernel,
        out_shape=out_shape,
        in_specs=in_specs,
        out_specs=out_specs,
        scratch_shapes=scratch,
        compiler_params=pltpu.CompilerParams(
            collective_id=ident,
            has_side_effects=ident is not None,
            vmem_limit_bytes=mib * 2**20,
        ),
        cost_estimate=pl.CostEstimate(flops=flops, bytes_accessed=2**23, transcendentals=0),
        name=kernel.__name__,
    )


def doc_table(lengths, tenants, prompt_len, token_pos):
    starts = jnp.cumsum(lengths) - lengths
    covered = (starts[None, :] <= token_pos[:, None]).astype(jnp.int32)
    doc_ids = jnp.sum(covered, axis=1) - 1
    onehot = (doc_ids[:, None] == jnp.arange(lengths.shape[0], dtype=jnp.int32)[None, :]).astype(jnp.int32)
    doc_begin = jnp.sum(onehot * starts[None, :], axis=1)
    tenant = jnp.sum(onehot * tenants[None, :], axis=1)
    head_len = jnp.sum(onehot * prompt_len[None, :], axis=1)
    within = token_pos - doc_begin
    return doc_begin, within, tenant, within < head_len


def body(hidden_in, prompt_table, norm_gain, w_qkv, w_out, doc_lengths, doc_tenant, prompt_lengths):
    s = lax.axis_index("seq")
    token_pos = s * POS + jnp.arange(POS, dtype=jnp.int32)
    table = jax.vmap(doc_table, in_axes=(0, 0, 0, None))
    begin, within, tenant, prompt = table(doc_lengths, doc_tenant, prompt_lengths, token_pos)
    flat_table = prompt_table.reshape(TENANTS * PLEN, FEAT)
    table_slot = tenant * PLEN + jnp.minimum(within, PLEN - 1)
    picker = (table_slot[..., None] == jnp.arange(TENANTS * PLEN, dtype=jnp.int32)).astype(BF16)
    lookup = jnp.einsum("rsk,kd->rsd", picker, flat_table, preferred_element_type=F32).astype(BF16)
    embedded = jnp.where(prompt[..., None], lookup, hidden_in)
    packed = [jnp.concatenate([embedded[r, :HALF], embedded[r, HALF:]], axis=1) for r in range(2)]

    half_dim = HEAD_DIM // 2
    inverse_freq = THETA ** (-jnp.arange(half_dim, dtype=F32) / half_dim)
    angles = within.astype(F32)[..., None] * inverse_freq
    cosine, sine = jnp.cos(angles), jnp.sin(angles)
    cos = jnp.concatenate([cosine, cosine], axis=2)
    sin = jnp.concatenate([-sine, sine], axis=2)
    gain = norm_gain.reshape(RING, 1, FEAT)
    owner = jnp.where(prompt, -1, tenant)[..., None]
    begin_col = begin[..., None]

    w_mine = jnp.pad(w_out, ((0, SLOT - SHARD), (0, 0))).reshape(SLOT, RING, FEAT)
    w_all = lax.all_gather(jnp.transpose(w_mine, (1, 0, 2)), "seq", axis=0)
    rows = np.arange(GROUP * HEAD_DIM)
    perm = np.zeros((GROUP * HEAD_DIM, DEPTH), np.float32)
    perm[rows, rows // SHARD * SLOT + rows % SHARD] = 1
    perm = jnp.asarray(perm, BF16)

    project_flops = 2 * POS * D * COLS
    q0, kv0 = call(
        project_kernel, 1, (Q_SHAPE, KV_SHAPE), [VM, VM, ANY, VM, VM], (VM, VM), FEATURE_SCRATCH, 40, project_flops
    )(packed[0], gain, w_qkv, cos[0], sin[0])
    q1, kv1, keys0 = call(
        project_keys_kernel, 2, (Q_SHAPE, KV_SHAPE, KEYS_SHAPE), [VM, VM, ANY, VM, VM, VM], (VM, VM, ANY),
        FEATURE_SCRATCH + KEY_SCRATCH, 40, project_flops,
    )(packed[1], gain, w_qkv, cos[1], sin[1], kv0)
    keys1 = call(keys_kernel, 3, KEYS_SHAPE, [VM], ANY, KEY_SCRATCH, 16, 2**20)(kv1)

    count = (s - begin[:, 0] // POS) // 2 + 1
    smem = pl.BlockSpec(memory_space=pltpu.SMEM)
    ctx0, ctx1 = call(
        attend_kernel, None, (CTX_SHAPE, CTX_SHAPE), [smem] + [VM] * 6, (VM, VM), ATTEND_SCRATCH, 48,
        8 * project_flops,
    )(count, q0, q1, keys0, keys1, begin_col[0], begin_col[1])

    out0, loss0 = call(
        sums_kernel, 4, (OUT_SHAPE, LOSS_SHAPE), [VM, VM, ANY, VM, VM], (VM, VM), SUM_SCRATCH, 40, project_flops
    )(ctx0, perm, w_all, packed[0], owner[0])
    loss_scratch = [
        pltpu.VMEM((3, RING, 8, HEAD_DIM), F32),
        pltpu.SemaphoreType.DMA((3, RING)),
        pltpu.SemaphoreType.DMA((3, RING)),
    ]
    out1, loss = call(
        last_kernel, 5, (OUT_SHAPE, LOSS_SHAPE), [VM, VM, ANY, VM, VM, VM], (VM, VM),
        SUM_SCRATCH + loss_scratch, 40, project_flops,
    )(ctx1, perm, w_all, packed[1], owner[1], loss0)
    return jnp.stack([out0, out1]), loss[0, :TENANTS]


def solution(mesh):
    placed = (
        P(None, "seq", "tensor"),
        P(None, None, "tensor"),
        P(),
        P(None, "tensor"),
        P(("tensor", "seq"), None),
        P(),
        P(),
        P(),
    )
    return jax.shard_map(
        body, mesh=mesh, in_specs=placed, out_specs=(P(None, "seq", "tensor"), P()), check_vma=False
    )
```

```python
import jax
import jax.numpy as jnp
import numpy as np
from jax import lax
from jax.experimental import pallas as pl
from jax.experimental.pallas import tpu as pltpu
from jax.sharding import PartitionSpec as P

D = 3584
HEAD_DIM = 128
GROUP = 7
TENANTS = 16
PLEN = 32
THETA = 5000000.0
EPS = 1e-05

DOCS = 16
SEQ = 32
RING = 8
POS = 256
FEAT = 448
HALF = POS // 2
WIDE = 2 * FEAT
SUB = HALF // 2
COLS = (GROUP + 2) * HEAD_DIM
SHARD = 28
SLOT = 32
DEPTH = SEQ * SLOT
WINDOW = 9
QSCALE = HEAD_DIM**-0.5 * 1.4426950408889634
LOW = -1e30
MESH = pl.DeviceIdType.MESH
F32 = jnp.float32
BF16 = jnp.bfloat16


def dot(a, b):
    return jnp.dot(a, b, preferred_element_type=F32)


def place():
    return lax.axis_index("seq"), lax.axis_index("tensor")


def ring_peers():
    s, z = place()
    return [(s, lax.rem(z + 1, RING)), (s, lax.rem(z + RING - 1, RING))]


def push(src, dst, send, recv, peer):
    return pltpu.make_async_remote_copy(
        src_ref=src, dst_ref=dst, send_sem=send, recv_sem=recv, device_id=peer, device_id_type=MESH
    )


def unpack(x):
    return jnp.concatenate([x[:, :FEAT], x[:, FEAT:]], axis=0)


def pack(x):
    return jnp.concatenate([x[:HALF], x[HALF:]], axis=1)


class Ring:
    def __init__(self, x, buf, send, recv):
        self.x, self.buf, self.send, self.recv = x, buf, send, recv
        self.z = place()[1]
        self.peers = ring_peers()

    def piece(self, way, hop, sub, mine):
        step = 1 if way == 0 else RING - 1
        origin = lax.rem(self.z + (RING - step) * (hop - 1 if mine else hop), RING)
        rows = pl.ds(sub * SUB, SUB)
        src = self.x.at[rows] if mine and hop == 1 else self.buf.at[origin, rows]
        index = (way, hop - 1, sub)
        return push(src, self.buf.at[origin, rows], self.send.at[index], self.recv.at[index], self.peers[way])

    def start(self):
        for sub in range(2):
            for way in range(2):
                self.piece(way, 1, sub, True).start()

    def relay(self, hop, sub):
        for way in range(2):
            if hop < 4 or sub == way:
                self.piece(way, hop, sub, False).wait_recv()
            if hop < 3 or (hop == 3 and sub == way):
                self.piece(way, hop + 1, sub, True).start()

    def block(self, away):
        origin = lax.rem(self.z + away, RING)
        return self.buf[origin], origin

    def drain(self):
        for hop in range(1, 5):
            for sub in range(2):
                for way in range(2):
                    if hop < 4 or sub == way:
                        self.piece(way, hop, sub, True).wait_send()


class Projection:
    def __init__(self, gain, w, wbuf, wsem, acc, ssq):
        self.gain, self.w = gain, w
        self.wbuf, self.wsem, self.acc, self.ssq = wbuf, wsem, acc, ssq

    def fetch(self):
        z = place()[1]
        for away in (0, 7, 1, 6, 2, 5, 3, 4):
            self.copy(lax.rem(z + away, RING)).start()

    def copy(self, origin):
        return pltpu.make_async_copy(
            self.w.at[pl.ds(origin * FEAT, FEAT)], self.wbuf.at[origin], self.wsem.at[origin]
        )

    def absorb(self, x, origin, fresh, first):
        if fresh:
            self.copy(origin).wait()
        wide = unpack(x).astype(F32)
        square = jnp.sum(wide * wide, axis=1, keepdims=True)
        scaled = (wide * self.gain[origin]).astype(BF16)
        product = dot(scaled, self.wbuf[origin])
        if first:
            self.ssq[...] = jnp.broadcast_to(square, self.ssq.shape)
            self.acc[...] = product
        else:
            self.ssq[...] += square
            self.acc[...] += product

    def finish(self, cos, sin, q, kv):
        scale = lax.rsqrt(self.ssq[...] / D + EPS)

        def rotated(n):
            part = self.acc[:, n * HEAD_DIM : (n + 1) * HEAD_DIM] * scale
            return part * cos[...] + pltpu.roll(part, HEAD_DIM // 2, 1) * sin[...]

        kv[:HEAD_DIM] = rotated(GROUP).T.astype(BF16)
        value = (self.acc[:, (GROUP + 1) * HEAD_DIM :] * scale).astype(BF16)
        kv[HEAD_DIM:] = pack(value)

        def queries():
            for n in range(GROUP):
                q[n] = (rotated(n) * QSCALE).astype(BF16)

        return queries


def plane_peers():
    s, z = place()
    x, y, c = s // 8, lax.rem(s // 2, 4), lax.rem(s, 2)

    def at(a, b):
        dx, dy = a * (1 - c) + b * c, a * c + b * (1 - c)
        return lax.rem(x + dx, 4) * 8 + lax.rem(y + dy, 4) * 2 + c

    return at, [(at(1, 0), z), (at(3, 0), z)], [(at(0, 1), z), (at(0, 3), z)], (s + 1 - 2 * c, z)


BACK = (3, 1)
KEY_SEMS = 36


class Plane:
    def __init__(self, own, everyone, send, recv, local):
        self.own, self.everyone, self.send, self.recv, self.local = own, everyone, send, recv, local
        at, self.first, self.second, self.sibling = plane_peers()
        self.s = place()[0]
        self.slots = {(a, b): at(a, b) for a in range(4) for b in range(4)}
        c = lax.rem(self.s, 2)
        x, y = self.s // 8, lax.rem(self.s // 2, 4)
        self.theirs = {}
        for a in range(4):
            for b in range(4):
                dx, dy = a * c + b * (1 - c), a * (1 - c) + b * c
                self.theirs[a, b] = lax.rem(x + dx, 4) * 8 + lax.rem(y + dy, 4) * 2 + 1 - c
        half = own.shape[0] // 2
        self.halves = (pl.ds(0, half), pl.ds(half, half))
        self.sent = {}

    def move(self, key, slot=None):
        kind, a, b, way = key
        rows = None
        if kind == "p1":
            index, peer = way, self.first[way]
        elif kind == "p2":
            index, peer, rows = 2 + way, self.first[way], self.halves[way]
        elif kind == "s1":
            index, peer = 4 + 4 * a + way, self.second[way]
        elif kind == "s2":
            index, peer, rows = 6 + 4 * a + way, self.second[way], self.halves[way]
        else:
            index, peer = 20 + 4 * a + b, self.sibling
        if slot is None:
            slot = self.slots[a, b]
        ref = self.everyone.at[slot, rows] if rows is not None else self.everyone.at[slot]
        src = self.own if (a, b) == (0, 0) and rows is None else ref
        return push(src, ref, self.send.at[index], self.recv.at[index], peer)

    def go(self, *key):
        self.sent[key] = True
        self.move(key).start()

    def await_(self, slot, *key):
        self.move(key, slot).wait_recv()

    def keep(self):
        return pltpu.make_async_copy(self.own, self.everyone.at[self.s], self.local)

    def start(self):
        self.keep().start()
        for way in range(2):
            self.go("p1", 0, 0, way)
        self.spread(0)

    def spread(self, a):
        for way in range(2):
            self.go("s1", a, 0, way)
        self.go("sib", a, 0, 0)

    def first_hop(self):
        for way in range(2):
            a = BACK[way]
            self.await_(self.slots[a, 0], "p1", 0, 0, way)
            self.go("p2", a, 0, way)
            self.spread(a)

    def second_hop(self):
        for way in range(2):
            self.await_(self.slots[2, 0], "p2", BACK[way], 0, way)
        self.spread(2)

    def cross(self, a):
        for way in range(2):
            b = BACK[way]
            self.await_(self.slots[a, b], "s1", a, 0, way)
            self.go("s2", a, b, way)
            self.go("sib", a, b, 0)

    def far(self, a):
        for way in range(2):
            self.await_(self.slots[a, 2], "s2", a, BACK[way], way)
        self.go("sib", a, 2, 0)

    def finish(self):
        for a in range(4):
            for b in range(4):
                self.await_(self.theirs[a, b], "sib", a, b, 0)
        self.keep().wait()

    def drain(self):
        for key in self.sent:
            self.move(key).wait_send()

    def steps(self):
        cross, far = self.cross, self.far
        return [
            self.first_hop, lambda: cross(0), self.second_hop, lambda: cross(3), lambda: cross(1),
            lambda: far(0), lambda: cross(2), lambda: far(3), lambda: far(1), lambda: far(2),
        ]


def attend(step, q, kv, begin, acc, top):
    s, _ = place()
    last = s - 2 * step
    low = jnp.maximum(last - 1, 0)
    key_pos = low * POS + lax.broadcasted_iota(jnp.int32, (POS, 2 * POS), 1)
    query_pos = s * POS + lax.broadcasted_iota(jnp.int32, (POS, 2 * POS), 0)
    allowed = (key_pos >= jnp.concatenate([begin] * 4, axis=1)) & (key_pos <= jnp.minimum(query_pos, last * POS + POS - 1))
    bias = jnp.where(allowed, 0.0, LOW)
    blocks = kv[pl.ds(low, 2)]
    keys = jnp.concatenate([blocks[0, :HEAD_DIM], blocks[1, :HEAD_DIM]], axis=1)
    values = [blocks[n, HEAD_DIM:, m * HEAD_DIM : (m + 1) * HEAD_DIM] for n in (0, 1) for m in (0, 1)]
    values = jnp.concatenate(values, axis=0)
    values = jnp.concatenate([values, jnp.ones_like(values)], axis=1)
    for n in range(GROUP):
        scores = dot(q[n], keys) + bias
        old = top[n]
        new = jnp.maximum(old, jnp.max(scores, axis=1, keepdims=True))
        weights = jnp.exp2(scores - jnp.concatenate([new] * 4, axis=1)).astype(BF16)
        rescale = jnp.exp2(old - new)
        acc[n] = acc[n] * jnp.concatenate([rescale] * 2, axis=1) + dot(weights, values)
        top[n] = new


def finish_attend(acc, ctx):
    for n in range(GROUP):
        both = acc[n]
        ctx[:, n * HEAD_DIM : (n + 1) * HEAD_DIM] = (both[:, :HEAD_DIM] / both[:, HEAD_DIM:]).astype(BF16)


class Sums:
    def __init__(self, wall, ctx, parts, out, came, send, recv):
        self.wall, self.ctx, self.parts = wall, ctx, parts
        self.out, self.came, self.send, self.recv = out, came, send, recv
        self.peers = ring_peers()
        self.z = place()[1]

    def part(self, away):
        owner = lax.rem(self.z + away, RING)
        odd = lax.rem(owner, 2)
        begin = pl.multiple_of(owner // 2 * WIDE + odd * (FEAT - 64), 128)
        w = self.wall[:, :, pl.ds(begin, 512)].reshape(DEPTH, 512)
        product = dot(self.ctx[...], w)
        product = jnp.where(odd == 1, product[:, 64:], product[:, :FEAT])
        return pack(product)

    def move(self, way, k, sub):
        rows = pl.ds(sub * SUB, SUB)
        index = (way, k, sub)
        return push(
            self.out.at[way, k, rows], self.came.at[way, k, rows],
            self.send.at[index], self.recv.at[index], self.peers[way],
        )

    def ship(self, way, k, sub, value):
        self.out[way, k, pl.ds(sub * SUB, SUB)] = value.astype(BF16)
        self.move(way, k, sub).start()

    def arrived(self, way, k, sub):
        self.move(way, k, sub).wait_recv()
        return self.came[way, k, pl.ds(sub * SUB, SUB)].astype(F32)

    def first(self):
        value = self.part(4)
        for way in range(2):
            self.ship(way, 0, way, value[way * SUB : (way + 1) * SUB])

    def ready(self, k):
        self.parts[0] = self.part(4 - k)
        self.parts[1] = self.part(4 + k)

    def turn(self, k, turn):
        for way in range(2):
            sub = 1 - (turn ^ way) if k == 1 else turn
            piece = self.parts[way, pl.ds(sub * SUB, SUB)]
            if k > 1 or sub == way:
                piece = piece + self.arrived(way, k - 1, sub)
            self.ship(way, k, sub, piece)

    def finish(self):
        self.parts[0] = self.part(0)
        for sub in range(2):
            rows = pl.ds(sub * SUB, SUB)
            self.parts[0, rows] = self.parts[0, rows] + self.arrived(0, 3, sub) + self.arrived(1, 3, sub)

    def drain(self):
        for way in range(2):
            for k in range(4):
                for sub in range(2):
                    if k > 0 or sub == way:
                        self.move(way, k, sub).wait_send()

    def steps(self):
        def both(k):
            self.ready(k)
            self.turn(k, 0)

        return [
            self.first,
            lambda: both(1), lambda: self.turn(1, 1),
            lambda: both(2), lambda: self.turn(2, 1),
            lambda: both(3), lambda: self.turn(3, 1),
        ]


def emit(delta, x, owner, out):
    delta = unpack(delta)
    out[...] = (unpack(x).astype(F32) + delta).astype(BF16)
    proxy = jnp.sum(delta * delta, axis=1, keepdims=True) / D
    lanes = lax.broadcasted_iota(jnp.int32, (POS, HEAD_DIM), 1)
    total = jnp.sum(jnp.where(owner[...] == lanes, proxy, 0.0), axis=0, keepdims=True)
    return jnp.broadcast_to(total, (8, HEAD_DIM))


def loss_groups():
    s, z = place()
    x, y, c = s // 8, lax.rem(s // 2, 4), lax.rem(s, 2)
    xc = x * 2 + c
    return [
        (z, 8, lambda n: (s, n)),
        (xc, 8, lambda n: ((n // 2) * 8 + y * 2 + lax.rem(n, 2), z)),
        (y, 4, lambda n: (x * 8 + n * 2 + c, z)),
    ]


def loss_peers():
    return [who(lax.rem(me + j, n)) for me, n, who in loss_groups() for j in range(1, n)]


def loss_total(value, slots, send, recv):
    for stage, (me, n, who) in enumerate(loss_groups()):
        slots[stage, me] = value
        sent = []
        for j in range(1, n):
            ref = slots.at[stage, me]
            copy = push(ref, ref, send.at[stage, j], recv.at[stage, j], who(lax.rem(me + j, n)))
            copy.start()
            sent.append(copy)
        for j in range(1, n):
            ref = slots.at[stage, lax.rem(me + n - j, n)]
            push(ref, ref, send.at[stage, j], recv.at[stage, j], who(lax.rem(me + j, n))).wait_recv()
        value = slots[stage, 0]
        for j in range(1, n):
            value = value + slots[stage, j]
        for copy in sent:
            copy.wait_send()
    return value


def describe(row, lengths, tenants, prompts):
    pos = place()[0] * POS + lax.broadcasted_iota(jnp.int32, (POS, HEAD_DIM), 0)
    begin = jnp.zeros_like(pos)
    tenant = jnp.full_like(pos, tenants[row, 0])
    prompt = jnp.full_like(pos, prompts[row, 0])
    start = jnp.int32(0)
    for doc in range(1, DOCS):
        start = start + lengths[row, doc - 1]
        inside = pos >= start
        begin = jnp.where(inside, start, begin)
        tenant = jnp.where(inside, tenants[row, doc], tenant)
        prompt = jnp.where(inside, prompts[row, doc], prompt)
    return begin, pos - begin, tenant, prompt


def embed(row, hidden, table, lengths, tenants, prompts, x, begin_ref, within_ref, owner_ref):
    begin, within, tenant, prompt = describe(row, lengths, tenants, prompts)
    begin_ref[row] = begin
    within_ref[row] = within
    owner_ref[row] = jnp.where(within < prompt, -1, tenant)
    slot = tenant * PLEN + jnp.minimum(within, PLEN - 1)
    entries = lax.broadcasted_iota(jnp.int32, (POS, TENANTS * PLEN), 1)
    picker = jnp.where(jnp.concatenate([slot] * 4, axis=1) == entries, 1.0, 0.0).astype(BF16)
    lookup = dot(picker, table[...])
    left = jnp.concatenate([prompt - within] * 4, axis=1)[:, :FEAT]
    x[row] = pack(jnp.where(left > 0, lookup, hidden[row].astype(F32)).astype(BF16))


def block_kernel(
    hidden, table, gain, w, w_out, lengths, tenants, prompts, freq, perm,
    out, loss,
    x, begin, within, owner, cos, sin, gains,
    wbuf, wsem, acc, ssq, buf0, buf1, fsend0, frecv0, fsend1, frecv1,
    q, own, keys0, keys1, ksend0, krecv0, ksend1, krecv1, klocal,
    wpad, wall, osend, orecv, olocal, permbuf, psem,
    total, top, ctx, mixed, parts,
    sout0, came0, ssend0, srecv0, sout1, came1, ssend1, srecv1,
    slots, lsend, lrecv,
):
    s, _ = place()
    peers = loss_peers()
    barrier = pltpu.get_barrier_semaphore()
    for peer in peers:
        pl.semaphore_signal(barrier, inc=1, device_id=peer, device_id_type=MESH)
    proj = Projection(gains, w, wbuf, wsem, acc, ssq)
    proj.fetch()
    perm_copy = pltpu.make_async_copy(perm, permbuf, psem)
    perm_copy.start()
    doc_refs = (lengths, tenants, prompts)
    embed(0, hidden, table, *doc_refs, x, begin, within, owner)
    wpad[:SHARD] = w_out[...]
    wpad[SHARD:] = jnp.zeros((SLOT - SHARD, D), BF16)
    for n in range(RING):
        gains[n] = gain[:, n * FEAT : (n + 1) * FEAT]
    pl.semaphore_wait(barrier, len(peers))

    ring = [Ring(x.at[0], buf0, fsend0, frecv0), Ring(x.at[1], buf1, fsend1, frecv1)]
    weights = Plane(wpad, wall, osend, orecv, olocal)
    keys = [
        Plane(own.at[0], keys0, ksend0, krecv0, klocal.at[0]),
        Plane(own.at[1], keys1, ksend1, krecv1, klocal.at[1]),
    ]
    sums = [
        Sums(wall, mixed, parts, sout0, came0, ssend0, srecv0),
        Sums(wall, mixed, parts, sout1, came1, ssend1, srecv1),
    ]

    def angles(row):
        angle = within[row].astype(F32) * freq[...]
        lane = lax.broadcasted_iota(jnp.int32, (POS, HEAD_DIM), 1)
        cos[row] = jnp.cos(angle)
        sine = jnp.sin(angle)
        sin[row] = jnp.where(lane < HEAD_DIM // 2, -sine, sine)

    def gather(row, between):
        between = list(between)

        def other(n=1):
            for _ in range(n):
                if between:
                    between.pop(0)()

        proj.absorb(x[row], place()[1], row == 0, True)
        other()
        for hop in range(1, 4):
            ring[row].relay(hop, 0)
            other()
            ring[row].relay(hop, 1)
            other()
            if hop == 3 and row == 0:
                ring[1].start()
            proj.absorb(*ring[row].block(RING - hop), row == 0, False)
            other()
            proj.absorb(*ring[row].block(hop), row == 0, False)
        for sub in range(2):
            ring[row].relay(4, sub)
        proj.absorb(*ring[row].block(4), row == 0, False)
        return between

    def queries_keys(row):
        queries = proj.finish(cos.at[row], sin.at[row], q.at[row], own.at[row])
        keys[row].start()
        queries()

    def attention(row, between):
        total[...] = jnp.zeros_like(total)
        top[...] = jnp.full_like(top, LOW)
        everyone = (keys0, keys1)[row]

        def step(n, carry):
            @pl.when(s >= 2 * n)
            def _():
                attend(n, q.at[row], everyone, begin[row], total, top)

            for at, one in enumerate(between):
                pl.when(n == at)(one)
            return carry

        lax.fori_loop(0, WINDOW, step, 0)
        finish_attend(total, ctx)

    ring[0].start()
    weights.start()
    embed(1, hidden, table, *doc_refs, x, begin, within, owner)
    angles(0)
    rest = gather(0, weights.steps()[:6] + [lambda: angles(1)])
    queries_keys(0)
    rest = rest + weights.steps()[6:]
    gather_steps = keys[0].steps()
    rest = gather(1, gather_steps[:6] + rest + gather_steps[6:])
    queries_keys(1)
    for one in rest:
        one()
    keys[0].finish()

    key_steps = keys[1].steps()
    attention(0, key_steps[:8] + [lambda: (key_steps[8](), key_steps[9]()) and None])
    weights.finish()
    keys[1].finish()
    perm_copy.wait()
    mixed[...] = dot(ctx[...], permbuf[...]).astype(BF16)
    attention(1, sums[0].steps())
    sums[0].finish()
    share = emit(parts[0], x[0], owner.at[0], out.at[0])
    mixed[...] = dot(ctx[...], permbuf[...]).astype(BF16)
    for one in sums[1].steps():
        one()
    sums[1].finish()
    share = share + emit(parts[0], x[1], owner.at[1], out.at[1])
    loss[...] = loss_total(share, slots, lsend, lrecv)
    for one in ring + [weights] + keys + sums:
        one.drain()


DMA = pltpu.SemaphoreType.DMA
RING_SEMS = DMA((2, 4, 2))
VM = pl.BlockSpec(memory_space=pltpu.VMEM)
SM = pl.BlockSpec(memory_space=pltpu.SMEM)
ANY = pl.BlockSpec(memory_space=pl.ANY)
SCRATCH = [
    pltpu.VMEM((2, HALF, WIDE), BF16),
    pltpu.VMEM((2, POS, HEAD_DIM), jnp.int32),
    pltpu.VMEM((2, POS, HEAD_DIM), jnp.int32),
    pltpu.VMEM((2, POS, HEAD_DIM), jnp.int32),
    pltpu.VMEM((2, POS, HEAD_DIM), F32),
    pltpu.VMEM((2, POS, HEAD_DIM), F32),
    pltpu.VMEM((RING, 1, FEAT), F32),
    pltpu.VMEM((RING, FEAT, COLS), BF16),
    DMA((RING,)),
    pltpu.VMEM((POS, COLS), F32),
    pltpu.VMEM((POS, HEAD_DIM), F32),
    pltpu.VMEM((RING, HALF, WIDE), BF16),
    pltpu.VMEM((RING, HALF, WIDE), BF16),
    RING_SEMS, RING_SEMS, RING_SEMS, RING_SEMS,
    pltpu.VMEM((2, GROUP, POS, HEAD_DIM), BF16),
    pltpu.VMEM((2, POS, 2 * HEAD_DIM), BF16),
    pltpu.VMEM((SEQ, POS, 2 * HEAD_DIM), BF16),
    pltpu.VMEM((SEQ, POS, 2 * HEAD_DIM), BF16),
    DMA((KEY_SEMS,)), DMA((KEY_SEMS,)), DMA((KEY_SEMS,)), DMA((KEY_SEMS,)),
    DMA((2,)),
    pltpu.VMEM((SLOT, D), BF16),
    pltpu.VMEM((SEQ, SLOT, D), BF16),
    DMA((KEY_SEMS,)), DMA((KEY_SEMS,)), DMA,
    pltpu.VMEM((GROUP * HEAD_DIM, DEPTH), BF16),
    DMA,
    pltpu.VMEM((GROUP, POS, 2 * HEAD_DIM), F32),
    pltpu.VMEM((GROUP, POS, HEAD_DIM), F32),
    pltpu.VMEM((POS, GROUP * HEAD_DIM), BF16),
    pltpu.VMEM((POS, DEPTH), BF16),
    pltpu.VMEM((2, HALF, WIDE), F32),
    pltpu.VMEM((2, 4, HALF, WIDE), BF16), pltpu.VMEM((2, 4, HALF, WIDE), BF16), RING_SEMS, RING_SEMS,
    pltpu.VMEM((2, 4, HALF, WIDE), BF16), pltpu.VMEM((2, 4, HALF, WIDE), BF16), RING_SEMS, RING_SEMS,
    pltpu.VMEM((3, RING, 8, HEAD_DIM), F32),
    DMA((3, RING)),
    DMA((3, RING)),
]


def body(hidden_in, prompt_table, norm_gain, w_qkv, w_out, doc_lengths, doc_tenant, prompt_lengths):
    freq = THETA ** (-np.arange(HEAD_DIM // 2) / (HEAD_DIM // 2))
    freq = jnp.asarray(np.concatenate([freq, freq])[None], F32)
    rows = np.arange(GROUP * HEAD_DIM)
    perm = np.zeros((GROUP * HEAD_DIM, DEPTH), np.float32)
    perm[rows, rows // SHARD * SLOT + rows % SHARD] = 1
    out, loss = pl.pallas_call(
        block_kernel,
        out_shape=(jax.ShapeDtypeStruct((2, POS, FEAT), BF16), jax.ShapeDtypeStruct((8, HEAD_DIM), F32)),
        in_specs=[VM, VM, VM, ANY, VM, SM, SM, SM, VM, ANY],
        out_specs=(VM, VM),
        scratch_shapes=SCRATCH,
        compiler_params=pltpu.CompilerParams(
            collective_id=1, has_side_effects=True, vmem_limit_bytes=60 * 2**20
        ),
        cost_estimate=pl.CostEstimate(flops=2 * 10**10, bytes_accessed=2 * 10**7, transcendentals=10**7),
        name="block",
    )(
        hidden_in, prompt_table.reshape(TENANTS * PLEN, FEAT), norm_gain[None], w_qkv, w_out,
        doc_lengths, doc_tenant, prompt_lengths, freq, jnp.asarray(perm, BF16),
    )
    return out, loss[0, :TENANTS]


def solution(mesh):
    placed = (
        P(None, "seq", "tensor"),
        P(None, None, "tensor"),
        P(),
        P(None, "tensor"),
        P(("tensor", "seq"), None),
        P(),
        P(),
        P(),
    )
    return jax.shard_map(
        body, mesh=mesh, in_specs=placed, out_specs=(P(None, "seq", "tensor"), P()), check_vma=False
    )
```

```python
import jax
import jax.numpy as jnp
import numpy as np
from jax import lax
from jax.experimental import pallas as pl
from jax.experimental.pallas import tpu as pltpu
from jax.sharding import PartitionSpec as P

D = 3584
HEAD_DIM = 128
GROUP = 7
TENANTS = 16
PLEN = 32
THETA = 5000000.0
EPS = 1e-05

DOCS = 16
SEQ = 32
RING = 8
POS = 256
FEAT = 448
HALF = POS // 2
WIDE = 2 * FEAT
SUB = HALF // 2
PIECES = 2
PIECE = SUB // PIECES
COLS = (GROUP + 2) * HEAD_DIM
SHARD = 28
SLOT = 32
DEPTH = SEQ * SLOT
REACH = 17
QSCALE = HEAD_DIM**-0.5 * 1.4426950408889634
LOW = -1e30
MESH = pl.DeviceIdType.MESH
F32 = jnp.float32
BF16 = jnp.bfloat16


def dot(a, b):
    return jnp.dot(a, b, preferred_element_type=F32)


def place():
    return lax.axis_index("seq"), lax.axis_index("tensor")


def ring_peers():
    s, z = place()
    return [(s, lax.rem(z + 1, RING)), (s, lax.rem(z + RING - 1, RING))]


def push(src, dst, send, recv, peer):
    return pltpu.make_async_remote_copy(
        src_ref=src, dst_ref=dst, send_sem=send, recv_sem=recv, device_id=peer, device_id_type=MESH
    )


def unpack(x):
    return jnp.concatenate([x[:, :FEAT], x[:, FEAT:]], axis=0)


def pack(x):
    return jnp.concatenate([x[:HALF], x[HALF:]], axis=1)


class Ring:
    def __init__(self, x, buf, send, recv):
        self.x, self.buf, self.send, self.recv = x, buf, send, recv
        self.z = place()[1]
        self.peers = ring_peers()

    def piece(self, way, hop, at, mine):
        step = 1 if way == 0 else RING - 1
        origin = lax.rem(self.z + (RING - step) * (hop - 1 if mine else hop), RING)
        rows = pl.ds(at * PIECE, PIECE)
        src = self.x.at[rows] if mine and hop == 1 else self.buf.at[origin, rows]
        index = (way, hop - 1, at)
        return push(src, self.buf.at[origin, rows], self.send.at[index], self.recv.at[index], self.peers[way])

    def start(self):
        for at in range(2 * PIECES):
            for way in range(2):
                self.piece(way, 1, at, True).start()

    def relay(self, hop, sub):
        for at in range(sub * PIECES, (sub + 1) * PIECES):
            for way in range(2):
                if hop < 4 or sub == way:
                    self.piece(way, hop, at, False).wait_recv()
                if hop < 3 or (hop == 3 and sub == way):
                    self.piece(way, hop + 1, at, True).start()

    def block(self, away):
        origin = lax.rem(self.z + away, RING)
        return self.buf[origin], origin

    def drain(self):
        for hop in range(1, 5):
            for at in range(2 * PIECES):
                for way in range(2):
                    if hop < 4 or at // PIECES == way:
                        self.piece(way, hop, at, True).wait_send()


class Projection:
    def __init__(self, gain, w, wbuf, wsem, acc, ssq):
        self.gain, self.w = gain, w
        self.wbuf, self.wsem, self.acc, self.ssq = wbuf, wsem, acc, ssq

    def fetch(self):
        z = place()[1]
        for away in (0, 7, 1, 6, 2, 5, 3, 4):
            self.copy(lax.rem(z + away, RING)).start()

    def copy(self, origin):
        return pltpu.make_async_copy(
            self.w.at[pl.ds(origin * FEAT, FEAT)], self.wbuf.at[origin], self.wsem.at[origin]
        )

    def absorb(self, x, origin, fresh, first):
        if fresh:
            self.copy(origin).wait()
        wide = unpack(x).astype(F32)
        square = jnp.sum(wide * wide, axis=1, keepdims=True)
        scaled = (wide * self.gain[origin]).astype(BF16)
        product = dot(scaled, self.wbuf[origin])
        if first:
            self.ssq[...] = jnp.broadcast_to(square, self.ssq.shape)
            self.acc[...] = product
        else:
            self.ssq[...] += square
            self.acc[...] += product

    def finish(self, cos, sin, q, kv):
        scale = lax.rsqrt(self.ssq[...] / D + EPS)

        def rotated(n):
            part = self.acc[:, n * HEAD_DIM : (n + 1) * HEAD_DIM] * scale
            return part * cos[...] + pltpu.roll(part, HEAD_DIM // 2, 1) * sin[...]

        kv[:HEAD_DIM] = rotated(GROUP).T.astype(BF16)
        value = (self.acc[:, (GROUP + 1) * HEAD_DIM :] * scale).astype(BF16)
        kv[HEAD_DIM:] = pack(value)

        def queries():
            for n in range(GROUP):
                q[n] = (rotated(n) * QSCALE).astype(BF16)

        return queries


def plane_peers():
    s, z = place()
    x, y, c = s // 8, lax.rem(s // 2, 4), lax.rem(s, 2)

    def at(a, b):
        dx, dy = a * (1 - c) + b * c, a * c + b * (1 - c)
        return lax.rem(x + dx, 4) * 8 + lax.rem(y + dy, 4) * 2 + c

    return at, [(at(1, 0), z), (at(3, 0), z)], [(at(0, 1), z), (at(0, 3), z)], (s + 1 - 2 * c, z)


BACK = (3, 1)
KEY_SEMS = 36


class Plane:
    def __init__(self, own, everyone, send, recv, local):
        self.own, self.everyone, self.send, self.recv, self.local = own, everyone, send, recv, local
        at, self.first, self.second, self.sibling = plane_peers()
        self.s = place()[0]
        self.slots = {(a, b): at(a, b) for a in range(4) for b in range(4)}
        c = lax.rem(self.s, 2)
        x, y = self.s // 8, lax.rem(self.s // 2, 4)
        self.theirs = {}
        for a in range(4):
            for b in range(4):
                dx, dy = a * c + b * (1 - c), a * (1 - c) + b * c
                self.theirs[a, b] = lax.rem(x + dx, 4) * 8 + lax.rem(y + dy, 4) * 2 + 1 - c
        half = own.shape[0] // 2
        self.halves = (pl.ds(0, half), pl.ds(half, half))
        self.sent = {}

    def move(self, key, slot=None):
        kind, a, b, way = key
        rows = None
        if kind == "p1":
            index, peer = way, self.first[way]
        elif kind == "p2":
            index, peer, rows = 2 + way, self.first[way], self.halves[way]
        elif kind == "s1":
            index, peer = 4 + 4 * a + way, self.second[way]
        elif kind == "s2":
            index, peer, rows = 6 + 4 * a + way, self.second[way], self.halves[way]
        else:
            index, peer = 20 + 4 * a + b, self.sibling
        if slot is None:
            slot = self.slots[a, b]
        ref = self.everyone.at[slot, rows] if rows is not None else self.everyone.at[slot]
        src = self.own if (a, b) == (0, 0) and rows is None else ref
        return push(src, ref, self.send.at[index], self.recv.at[index], peer)

    def go(self, *key):
        self.sent[key] = True
        self.move(key).start()

    def await_(self, slot, *key):
        self.move(key, slot).wait_recv()

    def keep(self):
        return pltpu.make_async_copy(self.own, self.everyone.at[self.s], self.local)

    def start(self):
        self.keep().start()
        for way in range(2):
            self.go("p1", 0, 0, way)
        self.spread(0)

    def spread(self, a):
        for way in range(2):
            self.go("s1", a, 0, way)
        self.go("sib", a, 0, 0)

    def first_hop(self):
        for way in range(2):
            a = BACK[way]
            self.await_(self.slots[a, 0], "p1", 0, 0, way)
            self.go("p2", a, 0, way)
            self.spread(a)

    def second_hop(self):
        for way in range(2):
            self.await_(self.slots[2, 0], "p2", BACK[way], 0, way)
        self.spread(2)

    def cross(self, a):
        for way in range(2):
            b = BACK[way]
            self.await_(self.slots[a, b], "s1", a, 0, way)
            self.go("s2", a, b, way)
            self.go("sib", a, b, 0)

    def far(self, a):
        for way in range(2):
            self.await_(self.slots[a, 2], "s2", a, BACK[way], way)
        self.go("sib", a, 2, 0)

    def handed(self, *blocks):
        for a, b in blocks:
            self.await_(self.theirs[a, b], "sib", a, b, 0)

    def drain(self):
        for key in self.sent:
            self.move(key).wait_send()

    def mine(self):
        self.keep().wait()
        self.handed((0, 0))

    def near(self):
        self.first_hop()
        self.cross(0)
        self.handed((3, 0), (1, 0), (0, 3), (0, 1))

    def corners(self):
        self.cross(3)
        self.cross(1)
        self.far(0)
        self.handed((3, 3), (3, 1), (1, 3), (1, 1), (2, 0), (0, 2))

    def wings(self):
        self.far(3)
        self.far(1)

    def rest(self):
        self.far(2)
        self.handed((2, 1), (2, 3), (1, 2), (3, 2), (2, 2))

    def rest_of(self):
        self.far(2)
        self.handed(*((a, b) for a in range(4) for b in range(4)))
        self.keep().wait()


VISITS = (
    (0, 0), (0, 3), (3, 0), (0, 1), (1, 0),
    (3, 3), (3, 1), (2, 0), (0, 2), (1, 3), (1, 1),
    (2, 3), (3, 2), (2, 1), (1, 2), (2, 2),
)


def visit(n):
    s, _ = place()
    x, y = s // 8, lax.rem(s // 2, 4)
    dx, dy = jnp.int32(0), jnp.int32(0)
    for at, (stepx, stepy) in enumerate(VISITS):
        dx = dx + jnp.where(n == at, stepx, 0)
        dy = dy + jnp.where(n == at, stepy, 0)
    chip = lax.rem(x + dx, 4) * 4 + lax.rem(y + dy, 4)
    return chip, (2 * chip <= s) & (2 * chip + 1 >= s - REACH)


def attend(chip, q, kv, begin, acc, top, scores_ref, weights):
    s, _ = place()
    low = 2 * chip
    key_pos = low * POS + lax.broadcasted_iota(jnp.int32, (POS, 2 * POS), 1)
    query_pos = s * POS + lax.broadcasted_iota(jnp.int32, (POS, 2 * POS), 0)
    allowed = (key_pos >= jnp.concatenate([begin] * 4, axis=1)) & (key_pos <= query_pos)
    bias = jnp.where(allowed, 0.0, LOW)
    blocks = kv[pl.ds(low, 2)]
    keys = jnp.concatenate([blocks[0, :HEAD_DIM], blocks[1, :HEAD_DIM]], axis=1)
    values = [blocks[n, HEAD_DIM:, m * HEAD_DIM : (m + 1) * HEAD_DIM] for n in (0, 1) for m in (0, 1)]
    values = jnp.concatenate(values, axis=0)
    values = jnp.concatenate([values, jnp.ones_like(values)], axis=1)
    scores_ref[...] = dot(q[...].reshape(GROUP * POS, HEAD_DIM), keys)
    for n in range(GROUP):
        rows = slice(n * POS, (n + 1) * POS)
        scores = scores_ref[rows] + bias
        old = top[n]
        new = jnp.maximum(old, jnp.max(scores, axis=1, keepdims=True))
        weights[rows] = jnp.exp2(scores - jnp.concatenate([new] * 4, axis=1)).astype(BF16)
        acc[n] = acc[n] * jnp.concatenate([jnp.exp2(old - new)] * 2, axis=1)
        top[n] = new
    acc[...] = acc[...] + dot(weights[...], values).reshape(GROUP, POS, 2 * HEAD_DIM)


def finish_attend(acc, ctx):
    for n in range(GROUP):
        both = acc[n]
        ctx[:, n * HEAD_DIM : (n + 1) * HEAD_DIM] = (both[:, :HEAD_DIM] / both[:, HEAD_DIM:]).astype(BF16)


class Sums:
    def __init__(self, wall, ctx, parts, out, came, send, recv):
        self.wall, self.ctx, self.parts = wall, ctx, parts
        self.out, self.came, self.send, self.recv = out, came, send, recv
        self.peers = ring_peers()
        self.z = place()[1]

    def part(self, away):
        owner = lax.rem(self.z + away, RING)
        odd = lax.rem(owner, 2)
        begin = pl.multiple_of(owner // 2 * WIDE + odd * (FEAT - 64), 128)
        w = self.wall[:, :, pl.ds(begin, 512)].reshape(DEPTH, 512)
        product = dot(self.ctx[...], w)
        product = jnp.where(odd == 1, product[:, 64:], product[:, :FEAT])
        return pack(product)

    def move(self, way, k, at):
        rows = pl.ds(at * PIECE, PIECE)
        index = (way, k, at)
        return push(
            self.out.at[way, k, rows], self.came.at[way, k, rows],
            self.send.at[index], self.recv.at[index], self.peers[way],
        )

    def ship(self, way, k, at, value):
        self.out[way, k, pl.ds(at * PIECE, PIECE)] = value.astype(BF16)
        self.move(way, k, at).start()

    def arrived(self, way, k, at):
        self.move(way, k, at).wait_recv()
        return self.came[way, k, pl.ds(at * PIECE, PIECE)].astype(F32)

    def first(self):
        value = self.part(4)
        for at in range(2 * PIECES):
            self.ship(at // PIECES, 0, at, value[at * PIECE : (at + 1) * PIECE])

    def ready(self, k):
        self.parts[0] = self.part(4 - k)
        self.parts[1] = self.part(4 + k)

    def turn(self, k, turn):
        for n in range(PIECES):
            for way in range(2):
                sub = 1 - (turn ^ way) if k == 1 else turn
                at = sub * PIECES + n
                piece = self.parts[way, pl.ds(at * PIECE, PIECE)]
                if k > 1 or sub == way:
                    piece = piece + self.arrived(way, k - 1, at)
                self.ship(way, k, at, piece)

    def finish(self):
        self.parts[0] = self.part(0)
        for at in range(2 * PIECES):
            rows = pl.ds(at * PIECE, PIECE)
            self.parts[0, rows] = self.parts[0, rows] + self.arrived(0, 3, at) + self.arrived(1, 3, at)

    def drain(self):
        for way in range(2):
            for k in range(4):
                for at in range(2 * PIECES):
                    if k > 0 or at // PIECES == way:
                        self.move(way, k, at).wait_send()

    def both(self, k):
        self.ready(k)
        self.turn(k, 0)


def losses(delta, owner):
    proxy = jnp.sum(delta * delta, axis=1, keepdims=True) / D
    lanes = lax.broadcasted_iota(jnp.int32, (POS, HEAD_DIM), 1)
    total = jnp.sum(jnp.where(owner == lanes, proxy, 0.0), axis=0, keepdims=True)
    return jnp.broadcast_to(total, (8, HEAD_DIM))


def emit(delta, x, out):
    out[...] = (unpack(x).astype(F32) + delta).T.astype(BF16)


def loss_groups():
    s, z = place()
    chip, c = s // 2, lax.rem(s, 2)
    return [
        (z * 2 + c, lambda n: (2 * chip + lax.rem(n, 2), n // 2)),
        (chip, lambda n: (2 * n + c, z)),
    ]


def loss_peers():
    return [who(lax.rem(me + j, 16)) for me, who in loss_groups() for j in range(1, 16)]


def loss_total(value, slots, send, recv, between):
    copies = []
    for stage, (me, who) in enumerate(loss_groups()):
        slots[stage, me] = value

        def swap(j, origin):
            ref = slots.at[stage, origin]
            return push(ref, ref, send.at[stage, j], recv.at[stage, j], who(lax.rem(me + j, 16)))

        for j in range(1, 16):
            copy = swap(j, me)
            copy.start()
            copies.append(copy)
        if stage == 0:
            between()
        for j in range(1, 16):
            swap(j, lax.rem(me + 16 - j, 16)).wait_recv()
        value = slots[stage, 0]
        for j in range(1, 16):
            value = value + slots[stage, j]
    for copy in copies:
        copy.wait_send()
    return value


def describe(row, lengths, tenants, prompts):
    pos = place()[0] * POS + lax.broadcasted_iota(jnp.int32, (POS, HEAD_DIM), 0)
    begin = jnp.zeros_like(pos)
    tenant = jnp.full_like(pos, tenants[row, 0])
    prompt = jnp.full_like(pos, prompts[row, 0])
    start = jnp.int32(0)
    for doc in range(1, DOCS):
        start = start + lengths[row, doc - 1]
        inside = pos >= start
        begin = jnp.where(inside, start, begin)
        tenant = jnp.where(inside, tenants[row, doc], tenant)
        prompt = jnp.where(inside, prompts[row, doc], prompt)
    return begin, pos - begin, tenant, prompt


def embed(row, hidden, table, lengths, tenants, prompts, x, begin_ref, within_ref, owner_ref):
    begin, within, tenant, prompt = describe(row, lengths, tenants, prompts)
    begin_ref[row] = begin
    within_ref[row] = within
    owner_ref[row] = jnp.where(within < prompt, -1, tenant)
    slot = tenant * PLEN + jnp.minimum(within, PLEN - 1)
    entries = lax.broadcasted_iota(jnp.int32, (POS, TENANTS * PLEN), 1)
    picker = jnp.where(jnp.concatenate([slot] * 4, axis=1) == entries, 1.0, 0.0).astype(BF16)
    lookup = dot(picker, table[...])
    left = jnp.concatenate([prompt - within] * 4, axis=1)[:, :FEAT]
    x[row] = pack(jnp.where(left > 0, lookup, hidden[row].astype(F32).T).astype(BF16))


def block_kernel(
    hidden_any, table_any, gain, w, w_out, lengths, tenants, prompts, freq,
    out, loss,
    hidden, table, hsem, x, begin, within, owner, cos, sin, gains,
    wbuf, wsem, acc, ssq, buf0, buf1, fsend0, frecv0, fsend1, frecv1,
    q, own, keys0, keys1, ksend0, krecv0, ksend1, krecv1, klocal,
    wpad, wall, osend, orecv, olocal, permbuf,
    total, top, scores, weights_bf, ctx, mixed, parts,
    sout0, came0, ssend0, srecv0, sout1, came1, ssend1, srecv1,
    slots, lsend, lrecv,
):
    s, _ = place()
    peers = loss_peers()
    barrier = pltpu.get_barrier_semaphore()
    for peer in peers:
        pl.semaphore_signal(barrier, inc=1, device_id=peer, device_id_type=MESH)
    arriving = [pltpu.make_async_copy(hidden_any, hidden, hsem.at[0]), pltpu.make_async_copy(table_any, table, hsem.at[1])]
    for copy in arriving:
        copy.start()
    proj = Projection(gains, w, wbuf, wsem, acc, ssq)
    proj.fetch()
    doc_refs = (lengths, tenants, prompts)
    for copy in arriving:
        copy.wait()
    embed(0, hidden, table, *doc_refs, x, begin, within, owner)
    wpad[:SHARD] = w_out[...]
    wpad[SHARD:] = jnp.zeros((SLOT - SHARD, D), BF16)
    whole = jnp.concatenate([gain[n : n + 1] for n in range(D // 128)], axis=1)
    for n in range(RING):
        gains[n] = whole[:, n * FEAT : (n + 1) * FEAT]
    pl.semaphore_wait(barrier, len(peers))

    ring = [Ring(x.at[0], buf0, fsend0, frecv0), Ring(x.at[1], buf1, fsend1, frecv1)]
    weights = Plane(wpad, wall, osend, orecv, olocal)
    keys = [
        Plane(own.at[0], keys0, ksend0, krecv0, klocal.at[0]),
        Plane(own.at[1], keys1, ksend1, krecv1, klocal.at[1]),
    ]
    sums = [
        Sums(wall, mixed.at[0], parts.at[0], sout0, came0, ssend0, srecv0),
        Sums(wall, mixed.at[1], parts.at[1], sout1, came1, ssend1, srecv1),
    ]

    def spacing():
        column = lax.broadcasted_iota(jnp.int32, (GROUP * HEAD_DIM, DEPTH), 1)
        row = lax.broadcasted_iota(jnp.int32, (GROUP * HEAD_DIM, DEPTH), 0)
        inside = column & (SLOT - 1)
        hit = (row == (column >> 5) * SHARD + inside) & (inside < SHARD)
        permbuf[...] = jnp.where(hit, 1.0, 0.0).astype(BF16)

    def angles(row):
        angle = within[row].astype(F32) * freq[...]
        lane = lax.broadcasted_iota(jnp.int32, (POS, HEAD_DIM), 1)
        cos[row] = jnp.cos(angle)
        sine = jnp.sin(angle)
        sin[row] = jnp.where(lane < HEAD_DIM // 2, -sine, sine)

    def absorb(row, *steps):
        for away in steps:
            proj.absorb(*ring[row].block(away), row == 0, False)

    def projected(row):
        queries = proj.finish(cos.at[row], sin.at[row], q.at[row], own.at[row])
        keys[row].start()
        queries()

    def attention(row, beside):
        total[...] = jnp.zeros_like(total)
        top[...] = jnp.full_like(top, LOW)
        everyone = (keys0, keys1)[row]

        def step(n, carry):
            for at, steps in beside.items():

                @pl.when(n == at)
                def _(steps=steps):
                    for one in steps:
                        one()

            chip, useful = visit(n)

            @pl.when(useful)
            def _():
                attend(chip, q.at[row], everyone, begin[row], total, top, scores, weights_bf)

            return carry

        lax.fori_loop(0, len(VISITS), step, 0)
        finish_attend(total, ctx)
        mixed[row] = dot(ctx[...], permbuf[...]).astype(BF16)

    ring[0].start()
    weights.start()
    proj.absorb(x[0], place()[1], True, True)
    embed(1, hidden, table, *doc_refs, x, begin, within, owner)
    ring[0].relay(1, 0)
    angles(0)
    ring[0].relay(1, 1)
    weights.first_hop()
    weights.cross(0)
    absorb(0, 7, 1)
    ring[0].relay(2, 0)
    spacing()
    ring[0].relay(2, 1)
    weights.second_hop()
    absorb(0, 6, 2)
    ring[0].relay(3, 0)
    weights.cross(3)
    ring[0].relay(3, 1)
    ring[1].start()
    weights.cross(1)
    absorb(0, 5, 3)
    angles(1)
    weights.far(0)
    ring[0].relay(4, 0)
    ring[0].relay(4, 1)
    absorb(0, 4)
    projected(0)
    ring[1].relay(1, 0)
    weights.cross(2)

    k0, k1, w_, r = keys[0], keys[1], weights, ring[1]
    attention(0, {
        0: [k0.mine],
        1: [
            lambda: r.relay(1, 1), lambda: proj.absorb(x[1], place()[1], False, True),
            lambda: absorb(1, 7, 1), lambda: r.relay(2, 0), k0.near,
        ],
        3: [lambda: r.relay(2, 1), k0.second_hop],
        4: [lambda: absorb(1, 6, 2), lambda: r.relay(3, 0)],
        5: [k0.corners],
        6: [lambda: r.relay(3, 1), lambda: k0.cross(2)],
        7: [lambda: absorb(1, 5, 3), lambda: r.relay(4, 0), lambda: r.relay(4, 1),
            lambda: absorb(1, 4), lambda: projected(1)],
        8: [w_.wings],
        9: [k0.wings],
        11: [k0.rest],
        12: [w_.rest_of],
    })
    one, other = sums
    one.first()
    attention(1, {
        0: [k1.mine, lambda: one.both(1)],
        1: [k1.near],
        2: [lambda: one.turn(1, 1)],
        3: [k1.second_hop],
        4: [lambda: one.both(2)],
        5: [k1.corners],
        6: [lambda: k1.cross(2)],
        7: [lambda: one.turn(2, 1)],
        9: [lambda: one.both(3), k1.wings],
        11: [k1.rest],
        12: [lambda: one.turn(3, 1)],
    })
    other.first()
    other.both(1)
    one.finish()
    other.turn(1, 1)
    delta = unpack(one.parts[0])
    share = losses(delta, owner[0])
    emit(delta, x[0], out.at[0])
    for k in range(2, 4):
        other.both(k)
        other.turn(k, 1)
    other.finish()
    delta = unpack(other.parts[0])
    share = share + losses(delta, owner[1])
    result = loss_total(share, slots, lsend, lrecv, lambda: emit(delta, x[1], out.at[1]))
    loss[...] = result[:1, :TENANTS]
    for each in ring + [weights] + keys + sums:
        each.drain()


DMA = pltpu.SemaphoreType.DMA
RING_SEMS = DMA((2, 4, 2 * PIECES))
VM = pl.BlockSpec(memory_space=pltpu.VMEM)
SM = pl.BlockSpec(memory_space=pltpu.SMEM)
ANY = pl.BlockSpec(memory_space=pl.ANY)
SCRATCH = [
    pltpu.VMEM((2, FEAT, POS), BF16),
    pltpu.VMEM((TENANTS * PLEN, FEAT), BF16),
    DMA((2,)),
    pltpu.VMEM((2, HALF, WIDE), BF16),
    pltpu.VMEM((2, POS, HEAD_DIM), jnp.int32),
    pltpu.VMEM((2, POS, HEAD_DIM), jnp.int32),
    pltpu.VMEM((2, POS, HEAD_DIM), jnp.int32),
    pltpu.VMEM((2, POS, HEAD_DIM), F32),
    pltpu.VMEM((2, POS, HEAD_DIM), F32),
    pltpu.VMEM((RING, 1, FEAT), F32),
    pltpu.VMEM((RING, FEAT, COLS), BF16),
    DMA((RING,)),
    pltpu.VMEM((POS, COLS), F32),
    pltpu.VMEM((POS, HEAD_DIM), F32),
    pltpu.VMEM((RING, HALF, WIDE), BF16),
    pltpu.VMEM((RING, HALF, WIDE), BF16),
    RING_SEMS, RING_SEMS, RING_SEMS, RING_SEMS,
    pltpu.VMEM((2, GROUP, POS, HEAD_DIM), BF16),
    pltpu.VMEM((2, POS, 2 * HEAD_DIM), BF16),
    pltpu.VMEM((SEQ, POS, 2 * HEAD_DIM), BF16),
    pltpu.VMEM((SEQ, POS, 2 * HEAD_DIM), BF16),
    DMA((KEY_SEMS,)), DMA((KEY_SEMS,)), DMA((KEY_SEMS,)), DMA((KEY_SEMS,)),
    DMA((2,)),
    pltpu.VMEM((SLOT, D), BF16),
    pltpu.VMEM((SEQ, SLOT, D), BF16),
    DMA((KEY_SEMS,)), DMA((KEY_SEMS,)), DMA,
    pltpu.VMEM((GROUP * HEAD_DIM, DEPTH), BF16),
    pltpu.VMEM((GROUP, POS, 2 * HEAD_DIM), F32),
    pltpu.VMEM((GROUP, POS, HEAD_DIM), F32),
    pltpu.VMEM((GROUP * POS, 4 * HEAD_DIM), F32),
    pltpu.VMEM((GROUP * POS, 4 * HEAD_DIM), BF16),
    pltpu.VMEM((POS, GROUP * HEAD_DIM), BF16),
    pltpu.VMEM((2, POS, DEPTH), BF16),
    pltpu.VMEM((2, 2, HALF, WIDE), F32),
    pltpu.VMEM((2, 4, HALF, WIDE), BF16), pltpu.VMEM((2, 4, HALF, WIDE), BF16), RING_SEMS, RING_SEMS,
    pltpu.VMEM((2, 4, HALF, WIDE), BF16), pltpu.VMEM((2, 4, HALF, WIDE), BF16), RING_SEMS, RING_SEMS,
    pltpu.VMEM((2, 16, 8, HEAD_DIM), F32),
    DMA((2, 16)),
    DMA((2, 16)),
]


def body(hidden_in, prompt_table, norm_gain, w_qkv, w_out, doc_lengths, doc_tenant, prompt_lengths):
    freq = THETA ** (-np.arange(HEAD_DIM // 2) / (HEAD_DIM // 2))
    freq = jnp.asarray(np.concatenate([freq, freq])[None], F32)
    out, loss = pl.pallas_call(
        block_kernel,
        out_shape=(jax.ShapeDtypeStruct((2, FEAT, POS), BF16), jax.ShapeDtypeStruct((1, TENANTS), F32)),
        in_specs=[ANY, ANY, VM, ANY, VM, SM, SM, SM, VM],
        out_specs=(VM, VM),
        scratch_shapes=SCRATCH,
        compiler_params=pltpu.CompilerParams(
            collective_id=1, has_side_effects=True, vmem_limit_bytes=60 * 2**20
        ),
        cost_estimate=pl.CostEstimate(flops=2 * 10**10, bytes_accessed=2 * 10**7, transcendentals=10**7),
        name="block",
    )(
        jnp.transpose(hidden_in, (0, 2, 1)), prompt_table.reshape(TENANTS * PLEN, FEAT), norm_gain.reshape(D // 128, 128), w_qkv, w_out,
        doc_lengths, doc_tenant, prompt_lengths, freq,
    )
    return jnp.transpose(out, (0, 2, 1)), loss.reshape(TENANTS)


def solution(mesh):
    placed = (
        P(None, "seq", "tensor"),
        P(None, None, "tensor"),
        P(),
        P(None, "tensor"),
        P(("tensor", "seq"), None),
        P(),
        P(),
        P(),
    )
    return jax.shard_map(
        body, mesh=mesh, in_specs=placed, out_specs=(P(None, "seq", "tensor"), P()), check_vma=False
    )
```

```python
import jax
import jax.numpy as jnp
import numpy as np
from jax import lax
from jax.experimental import pallas as pl
from jax.experimental.pallas import tpu as pltpu
from jax.sharding import PartitionSpec as P

D = 3584
HEAD_DIM = 128
GROUP = 7
TENANTS = 16
PLEN = 32
THETA = 5000000.0
EPS = 1e-05

DOCS = 16
SEQ = 32
RING = 8
POS = 256
FEAT = 448
HALF = POS // 2
WIDE = 2 * FEAT
SUB = HALF // 2
PIECES = 2
PIECE = SUB // PIECES
COLS = (GROUP + 2) * HEAD_DIM
SHARD = 28
SLOT = 32
DEPTH = SEQ * SLOT
REACH = 17
QSCALE = HEAD_DIM**-0.5 * 1.4426950408889634
LOW = -1e30
MESH = pl.DeviceIdType.MESH
F32 = jnp.float32
BF16 = jnp.bfloat16


def dot(a, b):
    return jnp.dot(a, b, preferred_element_type=F32)


def place():
    return lax.axis_index("seq"), lax.axis_index("tensor")


def ring_peers():
    s, z = place()
    return [(s, lax.rem(z + 1, RING)), (s, lax.rem(z + RING - 1, RING))]


def push(src, dst, send, recv, peer):
    return pltpu.make_async_remote_copy(
        src_ref=src, dst_ref=dst, send_sem=send, recv_sem=recv, device_id=peer, device_id_type=MESH
    )


def unpack(x):
    return jnp.concatenate([x[:, :FEAT], x[:, FEAT:]], axis=0)


def pack(x):
    return jnp.concatenate([x[:HALF], x[HALF:]], axis=1)


class Ring:
    def __init__(self, x, buf, send, recv):
        self.x, self.buf, self.send, self.recv = x, buf, send, recv
        self.z = place()[1]
        self.peers = ring_peers()

    def piece(self, way, hop, at, mine):
        step = 1 if way == 0 else RING - 1
        origin = lax.rem(self.z + (RING - step) * (hop - 1 if mine else hop), RING)
        rows = pl.ds(at * PIECE, PIECE)
        src = self.x.at[rows] if mine and hop == 1 else self.buf.at[origin, rows]
        index = (way, hop - 1, at)
        return push(src, self.buf.at[origin, rows], self.send.at[index], self.recv.at[index], self.peers[way])

    def start(self):
        for at in range(2 * PIECES):
            for way in range(2):
                self.piece(way, 1, at, True).start()

    def relay(self, hop, sub):
        for at in range(sub * PIECES, (sub + 1) * PIECES):
            for way in range(2):
                if hop < 4 or sub == way:
                    self.piece(way, hop, at, False).wait_recv()
                if hop < 3 or (hop == 3 and sub == way):
                    self.piece(way, hop + 1, at, True).start()

    def block(self, away):
        origin = lax.rem(self.z + away, RING)
        return self.buf[origin], origin

    def drain(self):
        for hop in range(1, 5):
            for at in range(2 * PIECES):
                for way in range(2):
                    if hop < 4 or at // PIECES == way:
                        self.piece(way, hop, at, True).wait_send()


class Projection:
    def __init__(self, gain, w, wbuf, wsem, acc, ssq):
        self.gain, self.w = gain, w
        self.wbuf, self.wsem, self.acc, self.ssq = wbuf, wsem, acc, ssq

    def fetch(self):
        z = place()[1]
        for away in (0, 7, 1, 6, 2, 5, 3, 4):
            self.copy(lax.rem(z + away, RING)).start()

    def copy(self, origin):
        return pltpu.make_async_copy(
            self.w.at[pl.ds(origin * FEAT, FEAT)], self.wbuf.at[origin], self.wsem.at[origin]
        )

    def absorb(self, x, origin, fresh, first):
        if fresh:
            self.copy(origin).wait()
        wide = unpack(x).astype(F32)
        square = jnp.sum(wide * wide, axis=1, keepdims=True)
        scaled = (wide * self.gain[origin]).astype(BF16)
        product = dot(scaled, self.wbuf[origin])
        if first:
            self.ssq[...] = jnp.broadcast_to(square, self.ssq.shape)
            self.acc[...] = product
        else:
            self.ssq[...] += square
            self.acc[...] += product

    def finish(self, cos, sin, q, kv):
        scale = lax.rsqrt(self.ssq[...] / D + EPS)

        def rotated(n):
            part = self.acc[:, n * HEAD_DIM : (n + 1) * HEAD_DIM] * scale
            return part * cos[...] + pltpu.roll(part, HEAD_DIM // 2, 1) * sin[...]

        kv[:HEAD_DIM] = rotated(GROUP).T.astype(BF16)
        value = (self.acc[:, (GROUP + 1) * HEAD_DIM :] * scale).astype(BF16)
        kv[HEAD_DIM:] = pack(value)

        def queries():
            for n in range(GROUP):
                q[n] = (rotated(n) * QSCALE).astype(BF16)

        return queries


def plane_peers():
    s, z = place()
    x, y, c = s // 8, lax.rem(s // 2, 4), lax.rem(s, 2)

    def at(a, b):
        dx, dy = a * (1 - c) + b * c, a * c + b * (1 - c)
        return lax.rem(x + dx, 4) * 8 + lax.rem(y + dy, 4) * 2 + c

    return at, [(at(1, 0), z), (at(3, 0), z)], [(at(0, 1), z), (at(0, 3), z)], (s + 1 - 2 * c, z)


BACK = (3, 1)
KEY_SEMS = 36


class Plane:
    def __init__(self, own, everyone, send, recv, local):
        self.own, self.everyone, self.send, self.recv, self.local = own, everyone, send, recv, local
        at, self.first, self.second, self.sibling = plane_peers()
        self.s = place()[0]
        self.slots = {(a, b): at(a, b) for a in range(4) for b in range(4)}
        c = lax.rem(self.s, 2)
        x, y = self.s // 8, lax.rem(self.s // 2, 4)
        self.theirs = {}
        for a in range(4):
            for b in range(4):
                dx, dy = a * c + b * (1 - c), a * (1 - c) + b * c
                self.theirs[a, b] = lax.rem(x + dx, 4) * 8 + lax.rem(y + dy, 4) * 2 + 1 - c
        half = own.shape[0] // 2
        self.halves = (pl.ds(0, half), pl.ds(half, half))
        self.sent = {}

    def move(self, key, slot=None):
        kind, a, b, way = key
        rows = None
        if kind == "p1":
            index, peer = way, self.first[way]
        elif kind == "p2":
            index, peer, rows = 2 + way, self.first[way], self.halves[way]
        elif kind == "s1":
            index, peer = 4 + 4 * a + way, self.second[way]
        elif kind == "s2":
            index, peer, rows = 6 + 4 * a + way, self.second[way], self.halves[way]
        else:
            index, peer = 20 + 4 * a + b, self.sibling
        if slot is None:
            slot = self.slots[a, b]
        ref = self.everyone.at[slot, rows] if rows is not None else self.everyone.at[slot]
        src = self.own if (a, b) == (0, 0) and rows is None else ref
        return push(src, ref, self.send.at[index], self.recv.at[index], peer)

    def go(self, *key):
        self.sent[key] = True
        self.move(key).start()

    def await_(self, slot, *key):
        self.move(key, slot).wait_recv()

    def keep(self):
        return pltpu.make_async_copy(self.own, self.everyone.at[self.s], self.local)

    def start(self):
        self.keep().start()
        for way in range(2):
            self.go("p1", 0, 0, way)
        self.spread(0)

    def spread(self, a):
        for way in range(2):
            self.go("s1", a, 0, way)
        self.go("sib", a, 0, 0)

    def first_hop(self):
        for way in range(2):
            a = BACK[way]
            self.await_(self.slots[a, 0], "p1", 0, 0, way)
            self.go("p2", a, 0, way)
            self.spread(a)

    def second_hop(self):
        for way in range(2):
            self.await_(self.slots[2, 0], "p2", BACK[way], 0, way)
        self.spread(2)

    def cross(self, a):
        for way in range(2):
            b = BACK[way]
            self.await_(self.slots[a, b], "s1", a, 0, way)
            self.go("s2", a, b, way)
            self.go("sib", a, b, 0)

    def far(self, a):
        for way in range(2):
            self.await_(self.slots[a, 2], "s2", a, BACK[way], way)
        self.go("sib", a, 2, 0)

    def handed(self, *blocks):
        for a, b in blocks:
            self.await_(self.theirs[a, b], "sib", a, b, 0)

    def drain(self):
        for key in self.sent:
            self.move(key).wait_send()

    def mine(self):
        self.keep().wait()
        self.handed((0, 0))

    def near(self):
        self.first_hop()
        self.cross(0)
        self.handed((3, 0), (1, 0), (0, 3), (0, 1))

    def corners(self):
        self.cross(3)
        self.cross(1)
        self.far(0)
        self.handed((3, 3), (3, 1), (1, 3), (1, 1), (2, 0), (0, 2))

    def wings(self):
        self.far(3)
        self.far(1)

    def rest(self):
        self.far(2)
        self.handed((2, 1), (2, 3), (1, 2), (3, 2), (2, 2))

    def rest_of(self):
        self.far(2)
        self.handed(*((a, b) for a in range(4) for b in range(4)))
        self.keep().wait()


VISITS = (
    (0, 0), (0, 3), (3, 0), (0, 1), (1, 0),
    (3, 3), (3, 1), (2, 0), (0, 2), (1, 3), (1, 1),
    (2, 3), (3, 2), (2, 1), (1, 2), (2, 2),
)


def visit(n):
    s, _ = place()
    x, y = s // 8, lax.rem(s // 2, 4)
    dx, dy = jnp.int32(0), jnp.int32(0)
    for at, (stepx, stepy) in enumerate(VISITS):
        dx = dx + jnp.where(n == at, stepx, 0)
        dy = dy + jnp.where(n == at, stepy, 0)
    chip = lax.rem(x + dx, 4) * 4 + lax.rem(y + dy, 4)
    inside = [(2 * chip + c <= s) & (2 * chip + c >= s - REACH) for c in range(2)]
    return chip, inside[0], inside[1]


def attend(low, count, q, kv, begin, acc, top, scores_ref, weights):
    s, _ = place()
    span = count * POS
    key_pos = low * POS + lax.broadcasted_iota(jnp.int32, (POS, span), 1)
    query_pos = s * POS + lax.broadcasted_iota(jnp.int32, (POS, span), 0)
    allowed = (key_pos >= jnp.concatenate([begin] * (2 * count), axis=1)) & (key_pos <= query_pos)
    bias = jnp.where(allowed, 0.0, LOW)
    blocks = [kv[low + n] for n in range(count)]
    keys = jnp.concatenate([block[:HEAD_DIM] for block in blocks], axis=1)
    values = [block[HEAD_DIM:, m * HEAD_DIM : (m + 1) * HEAD_DIM] for block in blocks for m in (0, 1)]
    values = jnp.concatenate(values, axis=0)
    values = jnp.concatenate([values, jnp.ones_like(values)], axis=1)
    scores_ref[:, :span] = dot(q[...].reshape(GROUP * POS, HEAD_DIM), keys)
    for n in range(GROUP):
        rows = slice(n * POS, (n + 1) * POS)
        scores = scores_ref[rows, :span] + bias
        old = top[n]
        new = jnp.maximum(old, jnp.max(scores, axis=1, keepdims=True))
        weights[rows, :span] = jnp.exp2(scores - jnp.concatenate([new] * (2 * count), axis=1)).astype(BF16)
        acc[n] = acc[n] * jnp.concatenate([jnp.exp2(old - new)] * 2, axis=1)
        top[n] = new
    acc[...] = acc[...] + dot(weights[:, :span], values).reshape(GROUP, POS, 2 * HEAD_DIM)


def finish_attend(acc, ctx):
    for n in range(GROUP):
        both = acc[n]
        ctx[:, n * HEAD_DIM : (n + 1) * HEAD_DIM] = (both[:, :HEAD_DIM] / both[:, HEAD_DIM:]).astype(BF16)


class Sums:
    def __init__(self, wall, ctx, parts, out, came, send, recv):
        self.wall, self.ctx, self.parts = wall, ctx, parts
        self.out, self.came, self.send, self.recv = out, came, send, recv
        self.peers = ring_peers()
        self.z = place()[1]

    def part(self, away):
        owner = lax.rem(self.z + away, RING)
        odd = lax.rem(owner, 2)
        begin = pl.multiple_of(owner // 2 * WIDE + odd * (FEAT - 64), 128)
        w = self.wall[:, :, pl.ds(begin, 512)].reshape(DEPTH, 512)
        product = dot(self.ctx[...], w)
        product = jnp.where(odd == 1, product[:, 64:], product[:, :FEAT])
        return pack(product)

    def move(self, way, k, at):
        rows = pl.ds(at * PIECE, PIECE)
        index = (way, k, at)
        return push(
            self.out.at[way, k, rows], self.came.at[way, k, rows],
            self.send.at[index], self.recv.at[index], self.peers[way],
        )

    def ship(self, way, k, at, value):
        self.out[way, k, pl.ds(at * PIECE, PIECE)] = value.astype(BF16)
        self.move(way, k, at).start()

    def arrived(self, way, k, at):
        self.move(way, k, at).wait_recv()
        return self.came[way, k, pl.ds(at * PIECE, PIECE)].astype(F32)

    def first(self):
        value = self.part(4)
        for at in range(2 * PIECES):
            self.ship(at // PIECES, 0, at, value[at * PIECE : (at + 1) * PIECE])

    def ready(self, k):
        self.parts[0] = self.part(4 - k)
        self.parts[1] = self.part(4 + k)

    def turn(self, k, turn):
        for n in range(PIECES):
            for way in range(2):
                sub = 1 - (turn ^ way) if k == 1 else turn
                at = sub * PIECES + n
                piece = self.parts[way, pl.ds(at * PIECE, PIECE)]
                if k > 1 or sub == way:
                    piece = piece + self.arrived(way, k - 1, at)
                self.ship(way, k, at, piece)

    def finish(self):
        self.parts[0] = self.part(0)
        for at in range(2 * PIECES):
            rows = pl.ds(at * PIECE, PIECE)
            self.parts[0, rows] = self.parts[0, rows] + self.arrived(0, 3, at) + self.arrived(1, 3, at)

    def drain(self):
        for way in range(2):
            for k in range(4):
                for at in range(2 * PIECES):
                    if k > 0 or at // PIECES == way:
                        self.move(way, k, at).wait_send()

    def both(self, k):
        self.ready(k)
        self.turn(k, 0)


def losses(delta, owner):
    proxy = jnp.sum(delta * delta, axis=1, keepdims=True) / D
    lanes = lax.broadcasted_iota(jnp.int32, (POS, HEAD_DIM), 1)
    total = jnp.sum(jnp.where(owner == lanes, proxy, 0.0), axis=0, keepdims=True)
    return jnp.broadcast_to(total, (8, HEAD_DIM))


def emit(delta, x, out):
    out[...] = (unpack(x).astype(F32) + delta).T.astype(BF16)


def loss_groups():
    s, z = place()
    chip, c = s // 2, lax.rem(s, 2)
    return [
        (z * 2 + c, lambda n: (2 * chip + lax.rem(n, 2), n // 2)),
        (chip, lambda n: (2 * n + c, z)),
    ]


def loss_peers():
    return [who(lax.rem(me + j, 16)) for me, who in loss_groups() for j in range(1, 16)]


def loss_total(value, slots, send, recv, between):
    copies = []
    for stage, (me, who) in enumerate(loss_groups()):
        slots[stage, me] = value

        def swap(j, origin):
            ref = slots.at[stage, origin]
            return push(ref, ref, send.at[stage, j], recv.at[stage, j], who(lax.rem(me + j, 16)))

        for j in range(1, 16):
            copy = swap(j, me)
            copy.start()
            copies.append(copy)
        if stage == 0:
            between()
        else:
            for copy in copies[:15]:
                copy.wait_send()
        for j in range(1, 16):
            swap(j, lax.rem(me + 16 - j, 16)).wait_recv()
        value = slots[stage, 0]
        for j in range(1, 16):
            value = value + slots[stage, j]
    for copy in copies[15:]:
        copy.wait_send()
    return value


def describe(row, lengths, tenants, prompts):
    pos = place()[0] * POS + lax.broadcasted_iota(jnp.int32, (POS, HEAD_DIM), 0)
    begin = jnp.zeros_like(pos)
    tenant = jnp.full_like(pos, tenants[row, 0])
    prompt = jnp.full_like(pos, prompts[row, 0])
    start = jnp.int32(0)
    for doc in range(1, DOCS):
        start = start + lengths[row, doc - 1]
        inside = pos >= start
        begin = jnp.where(inside, start, begin)
        tenant = jnp.where(inside, tenants[row, doc], tenant)
        prompt = jnp.where(inside, prompts[row, doc], prompt)
    return begin, pos - begin, tenant, prompt


def embed(row, hidden, table, lengths, tenants, prompts, x, begin_ref, within_ref, owner_ref):
    begin, within, tenant, prompt = describe(row, lengths, tenants, prompts)
    begin_ref[row] = begin
    within_ref[row] = within
    owner_ref[row] = jnp.where(within < prompt, -1, tenant)
    slot = tenant * PLEN + jnp.minimum(within, PLEN - 1)
    entries = lax.broadcasted_iota(jnp.int32, (POS, TENANTS * PLEN), 1)
    picker = jnp.where(jnp.concatenate([slot] * 4, axis=1) == entries, 1.0, 0.0).astype(BF16)
    lookup = dot(picker, table[...])
    left = jnp.concatenate([prompt - within] * 4, axis=1)[:, :FEAT]
    x[row] = pack(jnp.where(left > 0, lookup, hidden[row].astype(F32).T).astype(BF16))


def block_kernel(
    hidden_any, table_any, gain_any, w, w_out, lengths_any, tenants_any, prompts_any, freq_any,
    out_any, loss_any,
    gain, lengths, tenants, prompts, freq, out, loss, osem,
    hidden, table, hsem, x, begin, within, owner, cos, sin, gains,
    wbuf, wsem, acc, ssq, buf0, buf1, fsend0, frecv0, fsend1, frecv1,
    q, own, keys0, keys1, ksend0, krecv0, ksend1, krecv1, klocal,
    wpad, wall, osend, orecv, olocal, permbuf,
    total, top, scores, weights_bf, ctx, mixed, parts,
    sout0, came0, ssend0, srecv0, sout1, came1, ssend1, srecv1,
    slots, lsend, lrecv,
):
    s, _ = place()
    peers = loss_peers()
    barrier = pltpu.get_barrier_semaphore()
    for peer in peers:
        pl.semaphore_signal(barrier, inc=1, device_id=peer, device_id_type=MESH)
    sources = (lengths_any, tenants_any, prompts_any, hidden_any, table_any, gain_any, freq_any)
    targets = (lengths, tenants, prompts, hidden, table, gain, freq)
    arriving = [
        pltpu.make_async_copy(src, dst, hsem.at[n]) for n, (src, dst) in enumerate(zip(sources, targets))
    ]
    for copy in arriving:
        copy.start()
    proj = Projection(gains, w, wbuf, wsem, acc, ssq)
    proj.fetch()
    doc_refs = (lengths, tenants, prompts)
    for copy in arriving:
        copy.wait()
    embed(0, hidden, table, *doc_refs, x, begin, within, owner)
    wpad[:SHARD] = w_out[...]
    wpad[SHARD:] = jnp.zeros((SLOT - SHARD, D), BF16)
    whole = jnp.concatenate([gain[n : n + 1] for n in range(D // 128)], axis=1)
    for n in range(RING):
        gains[n] = whole[:, n * FEAT : (n + 1) * FEAT]
    pl.semaphore_wait(barrier, len(peers))

    ring = [Ring(x.at[0], buf0, fsend0, frecv0), Ring(x.at[1], buf1, fsend1, frecv1)]
    weights = Plane(wpad, wall, osend, orecv, olocal)
    keys = [
        Plane(own.at[0], keys0, ksend0, krecv0, klocal.at[0]),
        Plane(own.at[1], keys1, ksend1, krecv1, klocal.at[1]),
    ]
    sums = [
        Sums(wall, mixed.at[0], parts.at[0], sout0, came0, ssend0, srecv0),
        Sums(wall, mixed.at[1], parts.at[1], sout1, came1, ssend1, srecv1),
    ]

    def spacing():
        column = lax.broadcasted_iota(jnp.int32, (GROUP * HEAD_DIM, DEPTH), 1)
        row = lax.broadcasted_iota(jnp.int32, (GROUP * HEAD_DIM, DEPTH), 0)
        inside = column & (SLOT - 1)
        hit = (row == (column >> 5) * SHARD + inside) & (inside < SHARD)
        permbuf[...] = jnp.where(hit, 1.0, 0.0).astype(BF16)

    def angles(row):
        angle = within[row].astype(F32) * freq[...]
        lane = lax.broadcasted_iota(jnp.int32, (POS, HEAD_DIM), 1)
        cos[row] = jnp.cos(angle)
        sine = jnp.sin(angle)
        sin[row] = jnp.where(lane < HEAD_DIM // 2, -sine, sine)

    def absorb(row, *steps):
        for away in steps:
            proj.absorb(*ring[row].block(away), row == 0, False)

    def projected(row):
        queries = proj.finish(cos.at[row], sin.at[row], q.at[row], own.at[row])
        keys[row].start()
        queries()

    def attention(row, beside):
        total[...] = jnp.zeros_like(total)
        top[...] = jnp.full_like(top, LOW)
        everyone = (keys0, keys1)[row]

        def step(n, carry):
            for at, steps in beside.items():

                @pl.when(n == at)
                def _(steps=steps):
                    for one in steps:
                        one()

            chip, even, odd = visit(n)
            state = (q.at[row], everyone, begin[row], total, top, scores, weights_bf)

            @pl.when(even & odd)
            def _():
                attend(2 * chip, 2, *state)

            @pl.when(even ^ odd)
            def _():
                attend(2 * chip + jnp.where(odd, 1, 0), 1, *state)

            return carry

        lax.fori_loop(0, len(VISITS), step, 0)
        finish_attend(total, ctx)
        mixed[row] = dot(ctx[...], permbuf[...]).astype(BF16)

    ring[0].start()
    weights.start()
    proj.absorb(x[0], place()[1], True, True)
    embed(1, hidden, table, *doc_refs, x, begin, within, owner)
    ring[0].relay(1, 0)
    angles(0)
    ring[0].relay(1, 1)
    weights.first_hop()
    weights.cross(0)
    absorb(0, 7, 1)
    ring[0].relay(2, 0)
    spacing()
    ring[0].relay(2, 1)
    weights.second_hop()
    absorb(0, 6, 2)
    ring[0].relay(3, 0)
    weights.cross(3)
    ring[0].relay(3, 1)
    ring[1].start()
    weights.cross(1)
    absorb(0, 5, 3)
    angles(1)
    weights.far(0)
    ring[0].relay(4, 0)
    ring[0].relay(4, 1)
    absorb(0, 4)
    projected(0)
    ring[1].relay(1, 0)
    weights.cross(2)

    k0, k1, w_, r = keys[0], keys[1], weights, ring[1]
    attention(0, {
        0: [k0.mine],
        1: [
            lambda: r.relay(1, 1), lambda: proj.absorb(x[1], place()[1], False, True),
            lambda: absorb(1, 7, 1), lambda: r.relay(2, 0), k0.near,
        ],
        3: [lambda: r.relay(2, 1), k0.second_hop],
        4: [lambda: absorb(1, 6, 2), lambda: r.relay(3, 0)],
        5: [k0.corners],
        6: [lambda: r.relay(3, 1), lambda: k0.cross(2)],
        7: [lambda: absorb(1, 5, 3), lambda: r.relay(4, 0), lambda: r.relay(4, 1),
            lambda: absorb(1, 4), lambda: projected(1)],
        8: [w_.wings],
        9: [k0.wings],
        11: [k0.rest],
        12: [w_.rest_of],
    })
    one, other = sums
    one.first()
    attention(1, {
        0: [k1.mine, lambda: one.both(1)],
        1: [k1.near],
        2: [lambda: one.turn(1, 1)],
        3: [k1.second_hop],
        4: [lambda: one.both(2)],
        5: [k1.corners],
        6: [lambda: k1.cross(2)],
        7: [lambda: one.turn(2, 1)],
        9: [lambda: one.both(3), k1.wings],
        11: [k1.rest],
        12: [lambda: one.turn(3, 1)],
    })
    other.first()
    other.both(1)
    one.finish()
    other.turn(1, 1)
    delta = unpack(one.parts[0])
    share = losses(delta, owner[0])
    emit(delta, x[0], out.at[0])
    leaving = [pltpu.make_async_copy(out.at[n], out_any.at[n], osem.at[n]) for n in range(2)]
    leaving.append(pltpu.make_async_copy(loss, loss_any, osem.at[2]))
    leaving[0].start()
    for each in ring:
        each.drain()
    other.both(2)
    weights.drain()
    other.turn(2, 1)
    for each in keys:
        each.drain()
    other.both(3)
    one.drain()
    other.turn(3, 1)
    other.finish()
    delta = unpack(other.parts[0])
    share = share + losses(delta, owner[1])

    def last_row():
        emit(delta, x[1], out.at[1])
        leaving[1].start()
        other.drain()

    result = loss_total(share, slots, lsend, lrecv, last_row)
    loss[...] = result[:1, :TENANTS]
    leaving[2].start()
    for copy in leaving:
        copy.wait()


DMA = pltpu.SemaphoreType.DMA
RING_SEMS = DMA((2, 4, 2 * PIECES))
VM = pl.BlockSpec(memory_space=pltpu.VMEM)
ANY = pl.BlockSpec(memory_space=pl.ANY)
SCRATCH = [
    pltpu.VMEM((D // 128, 128), F32),
    pltpu.SMEM((2, DOCS), jnp.int32),
    pltpu.SMEM((2, DOCS), jnp.int32),
    pltpu.SMEM((2, DOCS), jnp.int32),
    pltpu.VMEM((1, HEAD_DIM), F32),
    pltpu.VMEM((2, FEAT, POS), BF16),
    pltpu.VMEM((1, TENANTS), F32),
    DMA((3,)),
    pltpu.VMEM((2, FEAT, POS), BF16),
    pltpu.VMEM((TENANTS * PLEN, FEAT), BF16),
    DMA((7,)),
    pltpu.VMEM((2, HALF, WIDE), BF16),
    pltpu.VMEM((2, POS, HEAD_DIM), jnp.int32),
    pltpu.VMEM((2, POS, HEAD_DIM), jnp.int32),
    pltpu.VMEM((2, POS, HEAD_DIM), jnp.int32),
    pltpu.VMEM((2, POS, HEAD_DIM), F32),
    pltpu.VMEM((2, POS, HEAD_DIM), F32),
    pltpu.VMEM((RING, 1, FEAT), F32),
    pltpu.VMEM((RING, FEAT, COLS), BF16),
    DMA((RING,)),
    pltpu.VMEM((POS, COLS), F32),
    pltpu.VMEM((POS, HEAD_DIM), F32),
    pltpu.VMEM((RING, HALF, WIDE), BF16),
    pltpu.VMEM((RING, HALF, WIDE), BF16),
    RING_SEMS, RING_SEMS, RING_SEMS, RING_SEMS,
    pltpu.VMEM((2, GROUP, POS, HEAD_DIM), BF16),
    pltpu.VMEM((2, POS, 2 * HEAD_DIM), BF16),
    pltpu.VMEM((SEQ, POS, 2 * HEAD_DIM), BF16),
    pltpu.VMEM((SEQ, POS, 2 * HEAD_DIM), BF16),
    DMA((KEY_SEMS,)), DMA((KEY_SEMS,)), DMA((KEY_SEMS,)), DMA((KEY_SEMS,)),
    DMA((2,)),
    pltpu.VMEM((SLOT, D), BF16),
    pltpu.VMEM((SEQ, SLOT, D), BF16),
    DMA((KEY_SEMS,)), DMA((KEY_SEMS,)), DMA,
    pltpu.VMEM((GROUP * HEAD_DIM, DEPTH), BF16),
    pltpu.VMEM((GROUP, POS, 2 * HEAD_DIM), F32),
    pltpu.VMEM((GROUP, POS, HEAD_DIM), F32),
    pltpu.VMEM((GROUP * POS, 4 * HEAD_DIM), F32),
    pltpu.VMEM((GROUP * POS, 4 * HEAD_DIM), BF16),
    pltpu.VMEM((POS, GROUP * HEAD_DIM), BF16),
    pltpu.VMEM((2, POS, DEPTH), BF16),
    pltpu.VMEM((2, 2, HALF, WIDE), F32),
    pltpu.VMEM((2, 4, HALF, WIDE), BF16), pltpu.VMEM((2, 4, HALF, WIDE), BF16), RING_SEMS, RING_SEMS,
    pltpu.VMEM((2, 4, HALF, WIDE), BF16), pltpu.VMEM((2, 4, HALF, WIDE), BF16), RING_SEMS, RING_SEMS,
    pltpu.VMEM((2, 16, 8, HEAD_DIM), F32),
    DMA((2, 16)),
    DMA((2, 16)),
]


def pass_kernel(out, loss, out_again, loss_again):
    out_again[...] = out[...]
    loss_again[...] = loss[...]


def body(hidden_in, prompt_table, norm_gain, w_qkv, w_out, doc_lengths, doc_tenant, prompt_lengths):
    freq = THETA ** (-np.arange(HEAD_DIM // 2) / (HEAD_DIM // 2))
    freq = jnp.asarray(np.concatenate([freq, freq])[None], F32)
    out, loss = pl.pallas_call(
        block_kernel,
        out_shape=(jax.ShapeDtypeStruct((2, FEAT, POS), BF16), jax.ShapeDtypeStruct((1, TENANTS), F32)),
        in_specs=[ANY, ANY, ANY, ANY, VM, ANY, ANY, ANY, ANY],
        out_specs=(ANY, ANY),
        scratch_shapes=SCRATCH,
        compiler_params=pltpu.CompilerParams(
            collective_id=1, has_side_effects=True, vmem_limit_bytes=60 * 2**20
        ),
        cost_estimate=pl.CostEstimate(flops=2 * 10**10, bytes_accessed=2 * 10**7, transcendentals=10**7),
        name="block",
    )(
        jnp.transpose(hidden_in, (0, 2, 1)), prompt_table.reshape(TENANTS * PLEN, FEAT), norm_gain.reshape(D // 128, 128), w_qkv, w_out,
        doc_lengths, doc_tenant, prompt_lengths, freq,
    )
    out, loss = pl.pallas_call(
        pass_kernel,
        out_shape=(jax.ShapeDtypeStruct((2, FEAT, POS), BF16), jax.ShapeDtypeStruct((1, TENANTS), F32)),
        in_specs=[VM, VM],
        out_specs=(VM, VM),
        name="hand_over",
    )(out, loss)
    return jnp.transpose(out, (0, 2, 1)), loss.reshape(TENANTS)


def solution(mesh):
    placed = (
        P(None, "seq", "tensor"),
        P(None, None, "tensor"),
        P(),
        P(None, "tensor"),
        P(("tensor", "seq"), None),
        P(),
        P(),
        P(),
    )
    return jax.shard_map(
        body, mesh=mesh, in_specs=placed, out_specs=(P(None, "seq", "tensor"), P()), check_vma=False
    )
```
